32 devices in a mesh: mem: 4 (over x, core), slab: 8 (over z, y).
Axes of the slice: x: 2, y: 2, z: 4, core: 2. Of those that a mesh axis runs over, the one named last changes fastest.
Arguments:
- prior_sample_group: bfloat16 [64, 32, 16, 1024], P('mem', None, 'slab'), may hold values from -6 to 6
- coefficients: float32 [3, 32, 16, 1024], P(None, None, 'slab'), may hold values from -0.3 to 0.3, as said below
- measured_quantity: float32 [32768], P('slab'), may hold values from -6 to 6
- measurement_precision: float32 [32768], P('slab'), may hold values from 0.5 to 4
- measurement_location: int32 [32768], P('slab'), may hold values from 0 to 65535
- obs_lists: int32 [16, 512, 128], P('slab', 'mem'), may hold values from 0 to 12287
- obs_counts: int32 [16, 512], P('slab', 'mem'), may hold values from 16 to 128, as said below
- loc_weight: float32 [16, 512, 128], P('slab', 'mem'), may hold values from 0.05 to 1
Outputs:
- analysis: bfloat16 [64, 32, 16, 1024], P(None, None, 'slab', 'mem')
The draws below stay inside these ranges and needn't reach their ends.
Inputs may be any that keep to these rules, and one draw needn't show every extreme that they name: `coefficients`: the third dimension's component 0 and 1 lie in [-0.3, 0.3], component 2 in [0.03, 0.15]. `measurement_location`: flattened index, level first, into the 32 x 2 x 1024 cells of the slab that holds the observation (observation o lies in slab o // 4096). `obs_lists`: an entry of a patch in row r indexes the observations of slabs r // 2 - 1, r // 2, r // 2 + 1 laid end to end, 4096 each; slots from obs_counts on are unused. `obs_counts`: in every block of patches held by one device some patch uses all 128 slots.
All inputs are finite; a program needn't handle non-finite values. Where the reference program divides by a largest or mean magnitude, that divisor is 1e-20 or more.
Results may differ from the reference program's by a relative error of at most 0.0051.
Values may be sent and summed in bfloat16 or wider, within the bound.
No kernel may reach another device: no remote copies, remote signals or barrier semaphores. Data moves between devices by JAX's collectives and lax.ppermute only.
A program may use at most 128 MiB of HBM per device.

```python
import math
import jax
import jax.numpy as jnp
from jax import lax

K = 64
MEM_DEV = 16
NZ = 32
CX = 2
NY = 1024
NX = 16
PCOL = 2
NOBS_DEV = 4096
NOBS = 32768
LMAX = 128
NS_ITERS = 4


def draw_coefficients(key, part):
    flow_key, mix_key = jax.random.split(key)
    flow = jax.random.uniform(flow_key, (2, NZ, NX, NY), jnp.float32, -0.3, 0.3)
    mixing = jax.random.uniform(mix_key, (1, NZ, NX, NY), jnp.float32, 0.0, 1.0)
    diffusion = 0.03 * jnp.exp(mixing * math.log(5.0))
    return jnp.concatenate([flow, diffusion], 0)


def draw_obs_counts(key, part):
    keys = jax.random.split(key, 5)
    slabs = NX // CX
    groups = K // MEM_DEV
    columns = NY // PCOL // groups
    dense = jax.random.randint(keys[0], (slabs, 1, 1, 1), 0, 8) == 0
    forced = jax.random.randint(keys[1], (), 0, slabs)
    dense = dense | (lax.broadcasted_iota(jnp.int32, (slabs, 1, 1, 1), 0) == forced)
    ceiling = jnp.where(dense, LMAX, LMAX // 3)
    counts = jax.random.randint(keys[2], (slabs, CX, groups, columns), LMAX // 8, ceiling + 1)
    pick_row = jax.random.randint(keys[3], (slabs, 1, groups, 1), 0, CX)
    pick_col = jax.random.randint(keys[4], (slabs, 1, groups, 1), 0, columns)
    rows_iota = lax.broadcasted_iota(jnp.int32, (slabs, CX, groups, columns), 1)
    cols_iota = lax.broadcasted_iota(jnp.int32, (slabs, CX, groups, columns), 3)
    chosen = (rows_iota == pick_row) & (cols_iota == pick_col)
    return jnp.where(chosen, LMAX, counts).reshape(NX, NY // PCOL)


def set_ends(values, key, low, top_value):
    longest = values.shape.index(max(values.shape))
    spots = []
    for shift in (0, 1):
        where = [jax.random.randint(jax.random.fold_in(key, axis), (), 0, length) for axis, length in enumerate(values.shape)]
        where[longest] = (where[longest] + shift) % values.shape[longest]
        spots.append(tuple(where))
    return values.at[spots[0]].set(low).at[spots[1]].set(top_value)


def steps_of(own_key, extent, cuts, smallest, largest):
    loudness = 1.0
    for dim, parts in cuts:
        draws = jax.random.uniform(jax.random.fold_in(jax.random.fold_in(own_key, 6), dim), (parts,), jnp.float32, smallest / len(cuts), largest / len(cuts))
        loudness = loudness * jnp.repeat(jnp.exp(draws), extent[dim] // parts).reshape((-1,) + (1,) * (len(extent) - 1 - dim))
    return loudness


def centred(stream_key, shape, scale, bound, cuts=(), kind=jnp.bfloat16):
    loudness = steps_of(stream_key, shape, cuts, -0.22, 0.18) if cuts else 1.0
    drawn = jax.random.normal(stream_key, shape, jnp.float32) * scale * loudness
    return jnp.minimum(jnp.maximum(drawn, -bound), bound).astype(kind)


def setup_inputs(seed: int = 0) -> dict:
    streams_of = jax.random.split(jax.random.key(seed), 9)
    prior_sample_group = centred(streams_of[0], (K, NZ, NX, NY), 1.0, 6.0, ((0, 4), (2, 8)))
    coefficients = draw_coefficients(jax.random.fold_in(streams_of[8], 71), 0)
    measured_quantity = centred(streams_of[2], (NOBS,), 1.0, 6.0, ((0, 8),), jnp.float32)
    measurement_precision = jnp.clip(jnp.exp(math.log(4.0) - 2.0794415 * jax.random.uniform(streams_of[3], (NOBS,), jnp.float32) ** steps_of(streams_of[3], (NOBS,), ((0, 8),), -0.2, 0.2)), 0.5, 4.0)
    measurement_location = set_ends(jax.random.randint(streams_of[4], (NOBS,), 0, NZ * CX * NY), jax.random.fold_in(streams_of[4], 1), 0, (NZ * CX * NY) - 1).astype(jnp.int32)
    obs_lists = set_ends(jax.random.randint(streams_of[5], (NX, NY // PCOL, LMAX), 0, 3 * NOBS_DEV), jax.random.fold_in(streams_of[5], 1), 0, (3 * NOBS_DEV) - 1).astype(jnp.int32)
    obs_counts = draw_obs_counts(jax.random.fold_in(streams_of[8], 71), 0)
    loc_weight = jnp.clip(jnp.exp(math.log(1.0) - 2.9957323 * jax.random.uniform(streams_of[7], (NX, NY // PCOL, LMAX), jnp.float32) ** steps_of(streams_of[7], (NX, NY // PCOL, LMAX), ((0, 8), (1, 4)), -0.2, 0.2)), 0.05, 1.0)
    return dict(prior_sample_group=prior_sample_group, coefficients=coefficients, measured_quantity=measured_quantity, measurement_precision=measurement_precision, measurement_location=measurement_location, obs_lists=obs_lists, obs_counts=obs_counts, loc_weight=loc_weight)


INFL = 1.1
HIGH = lax.Precision.HIGHEST

def stencil(padded, coeffs):
    center = padded[..., 1:-1, :]
    upper_row = padded[..., 2:, :]
    lower_row = padded[..., :-2, :]
    toward_east = jnp.roll(center, -1, axis=-1)
    toward_west = jnp.roll(center, 1, axis=-1)
    advect = coeffs[0] * (upper_row - lower_row) + coeffs[1] * (toward_east - toward_west)
    laplace = upper_row + lower_row + toward_east + toward_west - 4.0 * center
    return center - 0.5 * advect + coeffs[2] * laplace

def analyse(fields_row, picked, counts_row, weights_row):
    members = fields_row.shape[0]
    ensemble = picked[..., :members]
    observed = picked[..., members]
    inverse_var = picked[..., members + 1]
    position = lax.broadcasted_iota(jnp.int32, weights_row.shape, 1)
    weight = jnp.where(position < counts_row[:, None], weights_row * inverse_var, 0.0)
    obs_mean = lax.optimization_barrier(jnp.mean(ensemble, axis=-1))
    anomaly = ensemble - obs_mean[..., None]
    innovation = observed - obs_mean
    weighted = anomaly * weight[..., None]
    gram = jnp.einsum('plk,plm->pkm', weighted, anomaly, precision=HIGH)
    forcing = jnp.einsum('plk,pl->pk', weighted, innovation, precision=HIGH)
    inflated = (members - 1) / INFL
    ident = jnp.eye(members, dtype=jnp.float32)
    gershgorin = inflated + lax.optimization_barrier(jnp.max(lax.optimization_barrier(jnp.sum(jnp.abs(gram), axis=-1)), axis=-1))
    square = (inflated * ident + gram) / gershgorin[:, None, None]
    inverse = jnp.broadcast_to(ident, gram.shape)
    for sweep in range(NS_ITERS):
        factor = 1.5 * ident - 0.5 * jnp.einsum('pij,pjk->pik', inverse, square, precision=HIGH)
        square = jnp.einsum('pij,pjk->pik', square, factor, precision=HIGH)
        inverse = jnp.einsum('pij,pjk->pik', factor, inverse, precision=HIGH)
    inv_root = inverse / jnp.sqrt(gershgorin)[:, None, None]
    posterior = jnp.einsum('pij,pjk->pik', inv_root, inv_root, precision=HIGH)
    mean_shift = jnp.einsum('pjk,pk->pj', posterior, forcing, precision=HIGH)
    transform = math.sqrt(members - 1.0) * inv_root + mean_shift[:, :, None]
    state_row = fields_row.astype(jnp.float32)
    center = lax.optimization_barrier(jnp.mean(state_row, axis=0))
    deviation = state_row - center
    patches = transform.shape[0]
    levels = state_row.shape[1]
    blocks = deviation.reshape(members, levels, patches, -1)
    update = jnp.einsum('kzpc,pkm->mzpc', blocks, transform, precision=HIGH)
    return (center + update.reshape(members, levels, -1)).astype(jnp.bfloat16)

def reference(prior_sample_group, coefficients, measured_quantity, measurement_precision, measurement_location, obs_lists, obs_counts, loc_weight):
    slab_index = jnp.arange(NOBS, dtype=jnp.int32) // NOBS_DEV
    level = measurement_location // (CX * NY)
    within = measurement_location % (CX * NY)
    grid_row = slab_index * CX + within // NY
    flat_index = (level * NX + grid_row) * NY + within % NY

    def predicted_model_vector(realization_number):
        field = realization_number.astype(jnp.float32)
        for timestep in range(2):
            field = stencil(jnp.pad(field, ((0, 0), (1, 1), (0, 0))), coefficients)
        return (field.astype(jnp.bfloat16), jnp.take(field.reshape(-1), flat_index))
    model_variables, predicted_measurements = lax.map(predicted_model_vector, prior_sample_group)
    measurement_catalog = jnp.concatenate([predicted_measurements.T, measured_quantity[:, None], measurement_precision[:, None]], 1)

    def analyse_row(row_index):
        slab_row = row_index // CX
        lists_row = lax.dynamic_index_in_dim(obs_lists, row_index, 0, keepdims=False)
        global_index = slab_row * NOBS_DEV + lists_row - NOBS_DEV
        inside = (global_index >= 0) & (global_index < NOBS)
        picked = jnp.take(measurement_catalog, jnp.clip(global_index, 0, NOBS - 1), axis=0)
        picked = jnp.where(inside[..., None], picked, 0.0)
        fields_row = lax.dynamic_index_in_dim(model_variables, row_index, 2, keepdims=False)
        counts_row = lax.dynamic_index_in_dim(obs_counts, row_index, 0, keepdims=False)
        weights_row = lax.dynamic_index_in_dim(loc_weight, row_index, 0, keepdims=False)
        return analyse(fields_row, picked, counts_row, weights_row)
    result = lax.map(analyse_row, jnp.arange(NX, dtype=jnp.int32))
    return jnp.transpose(result, (1, 2, 0, 3))
```

```python
import functools
import math

import jax
import jax.numpy as jnp
from jax import lax
from jax.experimental import pallas as pl
from jax.experimental.pallas import tpu as pltpu
from jax.sharding import PartitionSpec as P

NS_ITERS = 4
INFL = 1.1
SHIFT = 1.25
LANES = 128
F32 = jnp.float32
BF16 = jnp.bfloat16
VMEM = pl.BlockSpec(memory_space=pltpu.VMEM)
SMEM = pl.BlockSpec(memory_space=pltpu.SMEM)


def params(mib):
    return pltpu.CompilerParams(vmem_limit_bytes=mib * 1024 * 1024)


def advance(upper, lower, center, c):
    width = center.shape[1]
    east = pltpu.roll(center, width - 1, 1)
    west = pltpu.roll(center, 1, 1)
    advect = c[0] * (upper - lower) + c[1] * (east - west)
    laplace = upper + lower + east + west - 4.0 * center
    return center - 0.5 * advect + c[2] * laplace


def forecast_kernel(groups, own_ref, prev_ref, next_ref, coef_ref, cprev_ref, cnext_ref, ship_ref, field_ref):
    levels, _, _, width = own_ref.shape
    part = width // groups

    def level(z, carry):
        rows = [prev_ref[z, 0], prev_ref[z, 1], own_ref[z, 0], own_ref[z, 1], next_ref[z, 0], next_ref[z, 1]]
        rows = [r.astype(F32) for r in rows]
        coeffs = [
            [cprev_ref[k, pl.ds(z, 1), :].astype(F32) for k in range(3)],
            [coef_ref[k, 0, pl.ds(z, 1), :] for k in range(3)],
            [coef_ref[k, 1, pl.ds(z, 1), :] for k in range(3)],
            [cnext_ref[k, pl.ds(z, 1), :].astype(F32) for k in range(3)],
        ]
        once = [advance(rows[i + 2], rows[i], rows[i + 1], coeffs[i]) for i in range(4)]
        for r in range(2):
            twice = advance(once[r + 2], once[r], once[r + 1], coeffs[r + 1]).astype(BF16)
            for g in range(groups):
                ship_ref[g, z, r] = twice[:, g * part : (g + 1) * part]
            for t in range(width // LANES):
                field_ref[(z * 2 + r) * (width // LANES) + t] = twice[:, t * LANES : (t + 1) * LANES]
        return carry

    lax.fori_loop(0, levels, level, 0)


def forecast(own, prev, following, coef, cprev, cnext, groups):
    levels, rows, members, width = own.shape
    return pl.pallas_call(
        functools.partial(forecast_kernel, groups),
        out_shape=[
            jax.ShapeDtypeStruct((groups, levels, rows, members, width // groups), BF16),
            jax.ShapeDtypeStruct((levels * rows * (width // LANES), members, LANES), BF16),
        ],
        in_specs=[VMEM] * 6,
        out_specs=[VMEM] * 2,
        compiler_params=params(48),
        name="forecast",
    )(own, prev, following, coef, cprev, cnext)


def observe_kernel(block_ref, shift_ref, field_ref, out_ref):
    count = out_ref.shape[0]
    members = out_ref.shape[1]
    lane = lax.broadcasted_iota(jnp.int32, (members, LANES), 1)

    def one(b, carry):
        acc = jnp.zeros((members, LANES), F32)
        for i in range(LANES):
            o = b * LANES + i
            tile = field_ref[block_ref[o]].astype(F32)
            acc = jnp.where(lane == i, pltpu.roll(tile, shift_ref[o], 1), acc)
        out_ref[b] = acc.astype(BF16)
        return carry

    lax.fori_loop(0, count, one, 0)


def observe(block, shift, field):
    members = field.shape[1]
    return pl.pallas_call(
        observe_kernel,
        out_shape=jax.ShapeDtypeStruct((block.shape[0] // LANES, members, LANES), BF16),
        in_specs=[SMEM, SMEM, VMEM],
        out_specs=VMEM,
        compiler_params=params(32),
        name="observe",
    )(block, shift, field)


def eye4():
    row = lax.broadcasted_iota(jnp.int32, (64, 256), 0)
    lane = lax.broadcasted_iota(jnp.int32, (64, 256), 1)
    return jnp.where(row == lane % 64, 1.0, 0.0).astype(F32)


def block_diag(x, low):
    left, right = x[:, :128], x[:, 128:]
    none = jnp.zeros_like(left)
    first, third = left * low, right * low
    top = jnp.concatenate([first, left - first, none, none], 0)
    bottom = jnp.concatenate([none, none, third, right - third], 0)
    return jnp.concatenate([top, bottom], 1)


def mul(a, b):
    return jnp.dot(a, b, preferred_element_type=F32)


def transform_kernel(unroll, slot_ref, lists_ref, ens_ref, obs_ref, wgt_ref, out_ref, cat_ref, rows_ref, sq_ref, force_ref, scale_ref):
    groups = slot_ref.shape[0]
    _, windows, blocks, per, _ = ens_ref.shape
    members = groups * per
    pairs = out_ref.shape[0]
    inflated = (members - 1) / INFL

    def catalog(i, carry):
        w, b = i // blocks, i % blocks
        ens = jnp.concatenate([ens_ref[slot_ref[j], w, b].astype(F32) for j in range(groups)], 0)
        mean = jnp.sum(ens, axis=0, keepdims=True) * (1.0 / members)
        value = obs_ref[w, 0, pl.ds(b, 1), :]
        root = jnp.sqrt(obs_ref[w, 1, pl.ds(b, 1), :])
        anomaly = (ens - mean) * root
        innovation = jnp.broadcast_to((value - mean) * root, ens.shape)
        cat_ref[pl.ds(pl.multiple_of(i * LANES, LANES), LANES), :] = jnp.concatenate([anomaly, innovation], 0).T
        return carry

    lax.fori_loop(0, windows * blocks, catalog, 0)

    ident = eye4()
    lane = lax.broadcasted_iota(jnp.int32, (64, 128), 1)
    lower = lane < 64

    def gather(g, carry):
        for half in range(2):
            q = g * 2 + half
            grams = []
            bounds = []
            for r in range(2):
                p = half * 2 + r
                for l in range(LANES):
                    rows_ref[p, pl.ds(l, 1), :] = cat_ref[pl.ds(lists_ref[r, q, l], 1), :]
                rows = rows_ref[p]
                weighted = rows.T[:64] * wgt_ref[r, pl.ds(q, 1), :]
                both = mul(weighted.astype(BF16), rows.astype(BF16))
                total = jnp.sum(jnp.where(lower, jnp.abs(both), 0.0), axis=0, keepdims=True)
                bounds.append(inflated + jnp.max(total, axis=1, keepdims=True))
                grams.append(both)
            turned = [pltpu.roll(x, 64, 1) for x in grams]
            bound = jnp.where(lower[:1], bounds[0], bounds[1])
            inv = 1.0 / bound
            gram = jnp.where(lower, grams[0], turned[1])
            force = jnp.where(lower, turned[0], grams[1])
            sl = slice(half * 128, half * 128 + 128)
            sq_ref[g, :, sl] = (gram + inflated * ident[:, :128]) * inv
            force_ref[g, :, sl] = force.astype(BF16)
            scale_ref[g, :, sl] = jnp.broadcast_to(inv, (8, 128))
        return carry

    lax.fori_loop(0, pairs, gather, 0)

    low = jnp.where(lane < 64, 1.0, 0.0).astype(BF16)

    def solve(s, carry):
        gs = [s * unroll + u for u in range(unroll)]
        n = range(unroll)
        sq = [sq_ref[g] for g in gs]
        h = [(1.5 - SHIFT) * ident - 0.5 * x for x in sq]
        inv = [SHIFT * ident + x for x in h]
        bd = [block_diag(x.astype(BF16), low) for x in h]
        sq = [SHIFT * sq[u] + mul(sq[u].astype(BF16), bd[u]) for u in n]
        for sweep in range(1, NS_ITERS):
            m = [mul(inv[u].astype(BF16), block_diag(sq[u].astype(BF16), low)) for u in n]
            bd = [block_diag(((1.5 - SHIFT) * ident - 0.5 * x).astype(BF16), low) for x in m]
            if sweep < NS_ITERS - 1:
                both = [jnp.concatenate([sq[u], inv[u]], 0) for u in n]
                both = [SHIFT * both[u] + mul(both[u].astype(BF16), bd[u]) for u in n]
                sq = [x[:64] for x in both]
                inv = [x[64:] for x in both]
            else:
                inv = [SHIFT * inv[u] + mul(inv[u].astype(BF16), bd[u]) for u in n]
        lhs = [x.astype(BF16) for x in inv]
        f = [mul(lhs[u], block_diag(force_ref[gs[u]], low)) for u in n]
        f = [mul(lhs[u], block_diag(f[u].astype(BF16), low)) for u in n]
        for u in n:
            scale = scale_ref[gs[u]][:1]
            out_ref[gs[u]] = (math.sqrt(members - 1.0) * jnp.sqrt(scale)) * inv[u] + scale * f[u]
        return carry

    lax.fori_loop(0, pairs // unroll, solve, 0)


def transforms(slots, lists, ens, obs, wgt):
    columns = lists.shape[1]
    pairs = columns // 2
    _, windows, blocks, _, _ = ens.shape
    return pl.pallas_call(
        functools.partial(transform_kernel, 4),
        out_shape=jax.ShapeDtypeStruct((pairs, 64, 256), F32),
        in_specs=[SMEM, SMEM, VMEM, VMEM, VMEM],
        out_specs=VMEM,
        scratch_shapes=[
            pltpu.VMEM((windows * blocks * LANES, LANES), F32),
            pltpu.VMEM((4, LANES, LANES), F32),
            pltpu.VMEM((pairs, 64, 256), F32),
            pltpu.VMEM((pairs, 64, 256), BF16),
            pltpu.VMEM((pairs, 8, 256), F32),
        ],
        compiler_params=params(48),
        name="transforms",
    )(slots, lists, ens, obs, wgt)


def update_kernel(state_ref, transform_ref, out_ref, cells_ref, center_ref):
    groups, levels, _, per, width = state_ref.shape
    members = groups * per
    pairs = transform_ref.shape[0]

    def enter(z, carry):
        parts = []
        for r in range(2):
            state = jnp.concatenate([state_ref[j, z, r].astype(F32) for j in range(groups)], 0)
            center = jnp.sum(state, axis=0, keepdims=True) * (1.0 / members)
            center_ref[z, pl.ds(r, 1), :] = center
            parts.append(state - center)
        cells_ref[pl.ds(pl.multiple_of(z * width, width), width), :] = jnp.concatenate(parts, 0).T
        return carry

    lax.fori_loop(0, levels, enter, 0)

    ident = eye4()
    lane = lax.broadcasted_iota(jnp.int32, (64, 128), 1)
    low = jnp.where(lane < 64, 1.0, 0.0).astype(BF16)

    def apply(g, carry):
        halves = []
        for half in range(2):
            q = g * 2 + half
            halves.append(jnp.concatenate([cells_ref[pl.ds(2 * q + c, levels, stride=width), :] for c in range(2)], 0))
        x = jnp.concatenate(halves, 1)
        t = transform_ref[g]
        on = t * ident
        diag = jnp.sum(on, axis=0, keepdims=True)
        y = x * diag + mul(x.astype(BF16), block_diag((t - on).astype(BF16), low))
        for half in range(2):
            q = g * 2 + half
            for c in range(2):
                cells_ref[pl.ds(2 * q + c, levels, stride=width), :] = y[c * levels : (c + 1) * levels, half * 128 : half * 128 + 128]
        return carry

    lax.fori_loop(0, pairs, apply, 0)

    def leave(z, carry):
        back = cells_ref[pl.ds(pl.multiple_of(z * width, width), width), :].T
        for r in range(2):
            out_ref[z, r] = (back[r * members : (r + 1) * members] + center_ref[z, pl.ds(r, 1), :]).astype(BF16)
        return carry

    lax.fori_loop(0, levels, leave, 0)


def update(state, transform):
    groups, levels, rows, per, width = state.shape
    return pl.pallas_call(
        update_kernel,
        out_shape=jax.ShapeDtypeStruct((levels, rows, groups * per, width), BF16),
        in_specs=[VMEM, VMEM],
        out_specs=VMEM,
        scratch_shapes=[
            pltpu.VMEM((levels * width, LANES), F32),
            pltpu.VMEM((levels, 8, width), F32),
        ],
        compiler_params=params(48),
        name="update",
    )(state, transform)


def bit_reversed(value, bits):
    return sum(((value >> b) & 1) << (bits - 1 - b) for b in range(bits))


def on_device(prior, coefficients, measured, precision, location, lists, counts, loc_weight):
    slabs = lax.axis_size("slab")
    groups = lax.axis_size("mem")
    bits = groups.bit_length() - 1
    me = lax.axis_index("mem")
    up = [(i, i + 1) for i in range(slabs - 1)]
    down = [(i + 1, i) for i in range(slabs - 1)]
    swap = [(i, i ^ 1) for i in range(slabs)]
    skip = [(i, i + 2) for i in range(0, slabs - 2, 2)] + [(i, i - 2) for i in range(3, slabs, 2)]
    odd = lax.axis_index("slab") % 2 == 1
    columns = prior.shape[3]
    nobs = measured.shape[0]

    own = jnp.transpose(prior, (1, 2, 0, 3))
    coef = jnp.transpose(coefficients, (0, 2, 1, 3))
    cprev = lax.ppermute(coef[:, 1].astype(BF16), "slab", up)
    cnext = lax.ppermute(coef[:, 0].astype(BF16), "slab", down)
    beside = lax.ppermute(own, "slab", swap)
    beyond = lax.ppermute(beside, "slab", skip)
    prev = jnp.where(odd, beside, beyond)
    following = jnp.where(odd, beyond, beside)
    ship, field = forecast(own, prev, following, coef, cprev.astype(F32), cnext.astype(F32), groups)

    zr, col = location // columns, location % columns
    block = zr * (columns // LANES) + col // LANES
    shift = (jnp.arange(nobs, dtype=jnp.int32) - col) % LANES
    seen = observe(block, shift, field)
    window = jnp.stack([lax.ppermute(seen, "slab", up), seen, lax.ppermute(seen, "slab", down)], 0)
    ens = window[None]
    step = groups // 2
    while step:
        ens = jnp.concatenate([ens, lax.ppermute(ens, "mem", [(i, i ^ step) for i in range(groups)])], 0)
        step //= 2
    slots = bit_reversed(jnp.arange(groups, dtype=jnp.int32) ^ me, bits)

    extras = jnp.stack([measured, precision], 0).reshape(2, nobs // LANES, LANES)
    obs = jnp.stack([lax.ppermute(extras, "slab", up), extras, lax.ppermute(extras, "slab", down)], 0)
    position = lax.broadcasted_iota(jnp.int32, loc_weight.shape, 2)
    wgt = jnp.where(position < counts[..., None], loc_weight, 0.0)
    transform = transforms(slots, lists, ens, obs, wgt)

    state = lax.all_to_all(ship, "mem", 0, 0, tiled=False)
    result = update(state, transform)
    return jnp.transpose(result, (2, 0, 1, 3))


def solution(mesh):
    return jax.shard_map(
        on_device,
        mesh=mesh,
        in_specs=(
            P("mem", None, "slab", None),
            P(None, None, "slab", None),
            P("slab"),
            P("slab"),
            P("slab"),
            P("slab", "mem", None),
            P("slab", "mem"),
            P("slab", "mem", None),
        ),
        out_specs=P(None, None, "slab", "mem"),
        check_vma=False,
    )
```

```python
import functools
import math

import jax
import jax.numpy as jnp
from jax import lax
from jax.experimental import pallas as pl
from jax.experimental.pallas import tpu as pltpu
from jax.sharding import PartitionSpec as P

NS_ITERS = 4
INFL = 1.1
SHIFT = 1.25
LANES = 128
F32 = jnp.float32
BF16 = jnp.bfloat16
VMEM = pl.BlockSpec(memory_space=pltpu.VMEM)
SMEM = pl.BlockSpec(memory_space=pltpu.SMEM)


def params(mib):
    return pltpu.CompilerParams(vmem_limit_bytes=mib * 1024 * 1024)


def advance(upper, lower, center, c):
    width = center.shape[1]
    east = pltpu.roll(center, width - 1, 1)
    west = pltpu.roll(center, 1, 1)
    advect = c[0] * (upper - lower) + c[1] * (east - west)
    laplace = upper + lower + east + west - 4.0 * center
    return center - 0.5 * advect + c[2] * laplace


def forecast_kernel(first, odd_ref, own_ref, beside_ref, beyond_ref, coef_ref, cprev_ref, cnext_ref, field_ref):
    levels, width = field_ref.shape[0], own_ref.shape[2]
    odd = odd_ref[0] == 1

    def level(z, carry):
        beside = [beside_ref[2 * z + r].astype(F32) for r in range(2)]
        beyond = [beyond_ref[2 * z + r].astype(F32) for r in range(2)]
        rows = [jnp.where(odd, beside[r], beyond[r]) for r in range(2)]
        rows += [own_ref[2 * z + r].astype(F32) for r in range(2)]
        rows += [jnp.where(odd, beyond[r], beside[r]) for r in range(2)]
        at = pl.ds(first + z, 1)
        coeffs = [
            [cprev_ref[k, at, :] for k in range(3)],
            [coef_ref[k, 0, at, :] for k in range(3)],
            [coef_ref[k, 1, at, :] for k in range(3)],
            [cnext_ref[k, at, :] for k in range(3)],
        ]
        once = [advance(rows[i + 2], rows[i], rows[i + 1], coeffs[i]) for i in range(4)]
        for r in range(2):
            twice = advance(once[r + 2], once[r], once[r + 1], coeffs[r + 1]).astype(BF16)
            for t in range(width // LANES):
                field_ref[z, r, t] = twice[:, t * LANES : (t + 1) * LANES]
        return carry

    lax.fori_loop(0, levels, level, 0)


def forecast(span, odd, own, beside, beyond, coef, cprev, cnext):
    first, levels, rows = span[0], span[1] - span[0], coef.shape[1]
    _, members, width = own.shape
    return pl.pallas_call(
        functools.partial(forecast_kernel, first),
        out_shape=jax.ShapeDtypeStruct((levels, rows, width // LANES, members, LANES), BF16),
        in_specs=[SMEM] + [VMEM] * 6,
        out_specs=VMEM,
        compiler_params=params(32),
        name="forecast",
    )(odd, own, beside, beyond, coef, cprev, cnext)


def observe_kernel(block_ref, shift_ref, *refs):
    *part_refs, out_ref, field_ref = refs
    first = 0
    for part in part_refs:
        field_ref[first : first + part.shape[0]] = part[...]
        first += part.shape[0]
    count = out_ref.shape[0]
    members = out_ref.shape[1]
    lane = lax.broadcasted_iota(jnp.int32, (members, LANES), 1)

    def one(b, carry):
        acc = jnp.zeros((members, LANES), F32)
        for i in range(LANES):
            o = b * LANES + i
            tile = field_ref[block_ref[o]].astype(F32)
            acc = jnp.where(lane == i, pltpu.roll(tile, shift_ref[o], 1), acc)
        out_ref[b] = acc.astype(BF16)
        return carry

    lax.fori_loop(0, count, one, 0)


def observe(block, shift, fields):
    parts = [f.reshape((-1,) + f.shape[3:]) for f in fields]
    members = parts[0].shape[1]
    return pl.pallas_call(
        observe_kernel,
        out_shape=jax.ShapeDtypeStruct((block.shape[0] // LANES, members, LANES), BF16),
        in_specs=[SMEM, SMEM] + [VMEM] * len(parts),
        out_specs=VMEM,
        scratch_shapes=[pltpu.VMEM((sum(p.shape[0] for p in parts), members, LANES), BF16)],
        compiler_params=params(32),
        name="observe",
    )(block, shift, *parts)


def eye4():
    row = lax.broadcasted_iota(jnp.int32, (64, 256), 0)
    lane = lax.broadcasted_iota(jnp.int32, (64, 256), 1)
    return jnp.where(row == lane % 64, 1.0, 0.0).astype(F32)


def block_diag(x, low):
    left, right = x[:, :128], x[:, 128:]
    none = jnp.zeros_like(left)
    first, third = left * low, right * low
    top = jnp.concatenate([first, left - first, none, none], 0)
    bottom = jnp.concatenate([none, none, third, right - third], 0)
    return jnp.concatenate([top, bottom], 1)


def mul(a, b):
    return jnp.dot(a, b, preferred_element_type=F32)


GROUPS = 4


def gather_block(lists_ref, wgt_ref, first, cat_ref, rows_ref, sq_ref, force_ref, scale_ref, ident, lower, inflated):
    for q in range(2 * GROUPS):
        grams = []
        bounds = []
        for r in range(2):
            p = (2 * q + r) % rows_ref.shape[0]
            for l in range(LANES):
                rows_ref[p, pl.ds(l, 1), :] = cat_ref[pl.ds(lists_ref[2 * q + r, l], 1), :]
            rows = rows_ref[p]
            weighted = rows.T[:64] * wgt_ref[r, pl.ds(first + q, 1), :]
            both = mul(weighted.astype(BF16), rows.astype(BF16))
            total = jnp.sum(jnp.where(lower, jnp.abs(both), 0.0), axis=0, keepdims=True)
            bounds.append(inflated + jnp.max(total, axis=1, keepdims=True))
            grams.append(both)
        turned = [pltpu.roll(x, 64, 1) for x in grams]
        inv = 1.0 / jnp.where(lower[:1], bounds[0], bounds[1])
        gram = jnp.where(lower, grams[0], turned[1])
        force = jnp.where(lower, turned[0], grams[1])
        g, half = q // 2, q % 2
        sl = slice(half * 128, half * 128 + 128)
        sq_ref[g, :, sl] = (gram + inflated * ident[:, :128]) * inv
        force_ref[g, :, sl] = force.astype(BF16)
        scale_ref[g, :, sl] = jnp.broadcast_to(inv, (8, 128))


def solve_block(sq_ref, force_ref, scale_ref, out_ref, first, ident, low, members):
    n = range(GROUPS)
    sq = [sq_ref[g] for g in n]
    h = [(1.5 - SHIFT) * ident - 0.5 * x for x in sq]
    inv = [SHIFT * ident + x for x in h]
    bd = [block_diag(x.astype(BF16), low) for x in h]
    sq = [SHIFT * sq[u] + mul(sq[u].astype(BF16), bd[u]) for u in n]
    for sweep in range(1, NS_ITERS):
        m = [mul(inv[u].astype(BF16), block_diag(sq[u].astype(BF16), low)) for u in n]
        bd = [block_diag(((1.5 - SHIFT) * ident - 0.5 * x).astype(BF16), low) for x in m]
        if sweep < NS_ITERS - 1:
            both = [jnp.concatenate([sq[u], inv[u]], 0) for u in n]
            both = [SHIFT * both[u] + mul(both[u].astype(BF16), bd[u]) for u in n]
            sq = [x[:64] for x in both]
            inv = [x[64:] for x in both]
        else:
            inv = [SHIFT * inv[u] + mul(inv[u].astype(BF16), bd[u]) for u in n]
    lhs = [x.astype(BF16) for x in inv]
    f = [mul(lhs[u], block_diag(force_ref[u], low)) for u in n]
    f = [mul(lhs[u], block_diag(f[u].astype(BF16), low)) for u in n]
    for u in n:
        scale = scale_ref[u][:1]
        out_ref[first + u] = (math.sqrt(members - 1.0) * jnp.sqrt(scale)) * inv[u] + scale * f[u]


def transform_kernel(slot_ref, ens_ref, obs_ref, wgt_ref, lists_ref, out_ref, cat_ref, rows_ref, *scratch):
    work, (lists_a, lists_b, sems) = (scratch[:3], scratch[3:6]), scratch[6:]
    smem = (lists_a, lists_b)
    groups = slot_ref.shape[0]
    _, windows, blocks, per, _ = ens_ref.shape
    members = groups * per
    count = lists_ref.shape[0]
    inflated = (members - 1) / INFL

    def fetch(b, half):
        return pltpu.make_async_copy(lists_ref.at[b], smem[half], sems.at[half])

    for half in range(2):
        fetch(half, half).start()

    def catalog(i, carry):
        w, b = i // blocks, i % blocks
        ens = jnp.concatenate([ens_ref[slot_ref[j], w, b].astype(F32) for j in range(groups)], 0)
        mean = jnp.sum(ens, axis=0, keepdims=True) * (1.0 / members)
        value = obs_ref[w, 0, pl.ds(b, 1), :]
        root = jnp.sqrt(obs_ref[w, 1, pl.ds(b, 1), :])
        anomaly = (ens - mean) * root
        innovation = jnp.broadcast_to((value - mean) * root, ens.shape)
        cat_ref[pl.ds(pl.multiple_of(i * LANES, LANES), LANES), :] = jnp.concatenate([anomaly, innovation], 0).T
        return carry

    lax.fori_loop(0, windows * blocks, catalog, 0, unroll=4)

    ident = eye4()
    lane = lax.broadcasted_iota(jnp.int32, (64, 128), 1)
    lower = lane < 64
    low = jnp.where(lower, 1.0, 0.0).astype(BF16)

    def pair(i, carry):
        for half in range(2):
            b = 2 * i + half
            fetch(b, half).wait()
            solve_block(*work[1 - half], out_ref, jnp.maximum(b - 1, 0) * GROUPS, ident, low, members)
            gather_block(smem[half], wgt_ref, b * 2 * GROUPS, cat_ref, rows_ref, *work[half], ident, lower, inflated)

            @pl.when(b + 2 < count)
            def _():
                fetch(b + 2, half).start()

        return carry

    lax.fori_loop(0, count // 2, pair, 0)
    solve_block(*work[1], out_ref, (count - 1) * GROUPS, ident, low, members)


def transforms(slots, lists, ens, obs, wgt):
    columns = lists.shape[1]
    pairs = columns // 2
    _, windows, blocks, _, _ = ens.shape
    lists = lists.reshape(2, pairs // GROUPS, 2 * GROUPS, LANES).transpose(1, 2, 0, 3).reshape(-1, 4 * GROUPS, LANES)
    work = [
        pltpu.VMEM((GROUPS, 64, 256), F32),
        pltpu.VMEM((GROUPS, 64, 256), BF16),
        pltpu.VMEM((GROUPS, 8, 256), F32),
    ]
    return pl.pallas_call(
        transform_kernel,
        out_shape=jax.ShapeDtypeStruct((pairs, 64, 256), F32),
        in_specs=[SMEM] + [VMEM] * 4,
        out_specs=VMEM,
        scratch_shapes=[
            pltpu.VMEM((windows * blocks * LANES, LANES), F32),
            pltpu.VMEM((8, LANES, LANES), F32),
            *work,
            *work,
            pltpu.SMEM((4 * GROUPS, LANES), jnp.int32),
            pltpu.SMEM((4 * GROUPS, LANES), jnp.int32),
            pltpu.SemaphoreType.DMA((2,)),
        ],
        compiler_params=params(48),
        name="transforms",
    )(slots, ens, obs, wgt, lists)


def update_kernel(state_ref, transform_ref, out_ref, cells_ref, moved_ref, center_ref):
    groups, levels, _, tiles, per, _ = state_ref.shape
    width = tiles * LANES
    members = groups * per
    pairs = transform_ref.shape[0]

    def enter(z, carry):
        parts = []
        for r in range(2):
            blocks = [[state_ref[j, z, r, t].astype(F32) for j in range(groups)] for t in range(tiles)]
            state = jnp.concatenate([jnp.concatenate(b, 0) for b in blocks], 1)
            center = jnp.sum(state, axis=0, keepdims=True) * (1.0 / members)
            center_ref[z, pl.ds(r, 1), :] = center
            parts.append(state - center)
        cells_ref[pl.ds(pl.multiple_of(z * width, width), width), :] = jnp.concatenate(parts, 0).T
        return carry

    lax.fori_loop(0, levels, enter, 0, unroll=4)

    ident = eye4()
    lane = lax.broadcasted_iota(jnp.int32, (64, 128), 1)
    low = jnp.where(lane < 64, 1.0, 0.0).astype(BF16)

    def apply(g, carry):
        halves = []
        for half in range(2):
            q = g * 2 + half
            halves.append(jnp.concatenate([cells_ref[pl.ds(2 * q + c, levels, stride=width), :] for c in range(2)], 0))
        x = jnp.concatenate(halves, 1)
        t = transform_ref[g]
        on = t * ident
        diag = jnp.sum(on, axis=0, keepdims=True)
        y = x * diag + mul(x.astype(BF16), block_diag((t - on).astype(BF16), low))
        for half in range(2):
            q = g * 2 + half
            for c in range(2):
                moved_ref[pl.ds(2 * q + c, levels, stride=width), :] = y[c * levels : (c + 1) * levels, half * 128 : half * 128 + 128]
        return carry

    lax.fori_loop(0, pairs, apply, 0, unroll=4)

    def leave(z, carry):
        back = moved_ref[pl.ds(pl.multiple_of(z * width, width), width), :].T
        for r in range(2):
            out_ref[z, r] = (back[r * members : (r + 1) * members] + center_ref[z, pl.ds(r, 1), :]).astype(BF16)
        return carry

    lax.fori_loop(0, levels, leave, 0, unroll=4)


def update(state, transform):
    groups, levels, rows, tiles, per, _ = state.shape
    width = tiles * LANES
    return pl.pallas_call(
        update_kernel,
        out_shape=jax.ShapeDtypeStruct((levels, rows, groups * per, width), BF16),
        in_specs=[VMEM, VMEM],
        out_specs=VMEM,
        scratch_shapes=[
            pltpu.VMEM((levels * width, LANES), F32),
            pltpu.VMEM((levels * width, LANES), F32),
            pltpu.VMEM((levels, 8, width), F32),
        ],
        compiler_params=params(48),
        name="update",
    )(state, transform)


def cuts(levels):
    eighth = levels // 8
    ends = [0, eighth, 3 * eighth, 5 * eighth, 7 * eighth, levels]
    return list(zip(ends[:-1], ends[1:]))


def bit_reversed(value, bits):
    return sum(((value >> b) & 1) << (bits - 1 - b) for b in range(bits))


def on_device(prior, coefficients, measured, precision, location, lists, counts, loc_weight):
    slabs = lax.axis_size("slab")
    groups = lax.axis_size("mem")
    bits = groups.bit_length() - 1
    me = lax.axis_index("mem")
    up = [(i, i + 1) for i in range(slabs - 1)]
    down = [(i + 1, i) for i in range(slabs - 1)]
    swap = [(i, i ^ 1) for i in range(slabs)]
    skip = [(i, i + 2) for i in range(0, slabs - 2, 2)] + [(i, i - 2) for i in range(3, slabs, 2)]
    odd = lax.axis_index("slab") % 2 == 1
    columns = prior.shape[3]
    nobs = measured.shape[0]

    levels, members = prior.shape[1], prior.shape[0]
    own = jnp.transpose(prior, (1, 2, 0, 3))
    coef = jnp.transpose(coefficients, (0, 2, 1, 3))
    spans = cuts(levels)
    pieces = [own[first:last].reshape(-1, members, columns) for first, last in spans]
    extra = coef.astype(BF16).reshape(-1, members, columns)
    pieces[0] = jnp.concatenate([pieces[0], extra], 0)
    pieces = lax.optimization_barrier(pieces)
    flag = odd.astype(jnp.int32).reshape(1)
    besides, beyonds, fields = [], [], []

    def advance_piece(i):
        nonlocal cprev, cnext
        if i == 0:
            sides = [x[0][-extra.shape[0] :].reshape(coef.shape).astype(F32) for x in (besides, beyonds)]
            cprev = jnp.where(odd, sides[0][:, 1], sides[1][:, 1])
            cnext = jnp.where(odd, sides[1][:, 0], sides[0][:, 0])
        fields.append(forecast(spans[i], flag, pieces[i], besides[i], beyonds[i], coef, cprev, cnext))

    cprev = cnext = None
    for i, piece in enumerate(pieces):
        if i >= 3:
            advance_piece(i - 3)
            fields[i - 3], piece = lax.optimization_barrier((fields[i - 3], piece))
        besides.append(lax.ppermute(piece, "slab", swap))
        if i >= 2:
            beyonds.append(lax.ppermute(besides[i - 2], "slab", skip))
    beyonds += [lax.ppermute(beside, "slab", skip) for beside in besides[-2:]]
    for i in range(len(fields), len(pieces)):
        advance_piece(i)

    zr, col = location // columns, location % columns
    block = zr * (columns // LANES) + col // LANES
    shift = (jnp.arange(nobs, dtype=jnp.int32) - col) % LANES
    seen = observe(block, shift, fields)
    extras = jnp.stack([measured, precision], 0)
    high = extras.astype(BF16)
    extras = jnp.concatenate([high, (extras - high.astype(F32)).astype(BF16)], 0)
    sent = jnp.concatenate([seen, extras.reshape((-1,) + seen.shape[1:])], 0)
    window = jnp.stack([lax.ppermute(sent, "slab", up), sent, lax.ppermute(sent, "slab", down)], 0)
    obs = window[:, seen.shape[0] :].reshape(3, 2, 2, nobs // LANES, LANES).astype(F32)
    obs = obs[:, 0] + obs[:, 1]
    window = window[:, : seen.shape[0]]
    ens = window[None]
    step = groups // 2
    while step:
        ens = jnp.concatenate([ens, lax.ppermute(ens, "mem", [(i, i ^ step) for i in range(groups)])], 0)
        step //= 2
    slots = bit_reversed(jnp.arange(groups, dtype=jnp.int32) ^ me, bits)

    position = lax.broadcasted_iota(jnp.int32, loc_weight.shape, 2)
    wgt = jnp.where(position < counts[..., None], loc_weight, 0.0)
    transform = transforms(slots, lists, ens, obs, wgt)

    tiles = columns // groups // LANES
    ship = jnp.concatenate(fields, 0)
    ship = ship.reshape(ship.shape[:2] + (groups, tiles) + ship.shape[3:])
    ship, _ = lax.optimization_barrier((jnp.transpose(ship, (2, 0, 1, 3, 4, 5)), ens))
    state = lax.all_to_all(ship, "mem", 0, 0, tiled=False)
    result = update(state, transform)
    return jnp.transpose(result, (2, 0, 1, 3))


def solution(mesh):
    return jax.shard_map(
        on_device,
        mesh=mesh,
        in_specs=(
            P("mem", None, "slab", None),
            P(None, None, "slab", None),
            P("slab"),
            P("slab"),
            P("slab"),
            P("slab", "mem", None),
            P("slab", "mem"),
            P("slab", "mem", None),
        ),
        out_specs=P(None, None, "slab", "mem"),
        check_vma=False,
    )
```

```python
import functools
import math

import jax
import jax.numpy as jnp
from jax import lax
from jax.experimental import pallas as pl
from jax.experimental.pallas import tpu as pltpu
from jax.sharding import PartitionSpec as P

NS_ITERS = 4
INFL = 1.1
SHIFT = 1.25
LANES = 128
F32 = jnp.float32
BF16 = jnp.bfloat16
VMEM = pl.BlockSpec(memory_space=pltpu.VMEM)
SMEM = pl.BlockSpec(memory_space=pltpu.SMEM)


def params(mib):
    return pltpu.CompilerParams(vmem_limit_bytes=mib * 1024 * 1024)


def advance(upper, lower, center, c):
    width = center.shape[1]
    east = pltpu.roll(center, width - 1, 1)
    west = pltpu.roll(center, 1, 1)
    advect = c[0] * (upper - lower) + c[1] * (east - west)
    laplace = upper + lower + east + west - 4.0 * center
    return center - 0.5 * advect + c[2] * laplace


def forecast_kernel(first, odd_ref, own_ref, beside_ref, beyond_ref, coef_ref, cprev_ref, cnext_ref, field_ref):
    levels, width = field_ref.shape[0], own_ref.shape[2]
    odd = odd_ref[0] == 1

    def level(z, carry):
        beside = [beside_ref[2 * z + r].astype(F32) for r in range(2)]
        beyond = [beyond_ref[2 * z + r].astype(F32) for r in range(2)]
        rows = [jnp.where(odd, beside[r], beyond[r]) for r in range(2)]
        rows += [own_ref[2 * z + r].astype(F32) for r in range(2)]
        rows += [jnp.where(odd, beyond[r], beside[r]) for r in range(2)]
        at = pl.ds(first + z, 1)
        coeffs = [
            [cprev_ref[k, at, :] for k in range(3)],
            [coef_ref[k, 0, at, :] for k in range(3)],
            [coef_ref[k, 1, at, :] for k in range(3)],
            [cnext_ref[k, at, :] for k in range(3)],
        ]
        once = [advance(rows[i + 2], rows[i], rows[i + 1], coeffs[i]) for i in range(4)]
        for r in range(2):
            twice = advance(once[r + 2], once[r], once[r + 1], coeffs[r + 1]).astype(BF16)
            for t in range(width // LANES):
                field_ref[z, r, t] = twice[:, t * LANES : (t + 1) * LANES]
        return carry

    lax.fori_loop(0, levels, level, 0)


def forecast(span, odd, own, beside, beyond, coef, cprev, cnext):
    first, levels, rows = span[0], span[1] - span[0], coef.shape[1]
    _, members, width = own.shape
    return pl.pallas_call(
        functools.partial(forecast_kernel, first),
        out_shape=jax.ShapeDtypeStruct((levels, rows, width // LANES, members, LANES), BF16),
        in_specs=[SMEM] + [VMEM] * 6,
        out_specs=VMEM,
        compiler_params=params(32),
        name="forecast",
    )(odd, own, beside, beyond, coef, cprev, cnext)


BATCH = 4


def observe_kernel(index_ref, *refs):
    *part_refs, out_ref, field_ref, smem_a, smem_b, sems = refs
    smem = (smem_a, smem_b)
    count = index_ref.shape[0]
    members = out_ref.shape[1]
    lane = lax.broadcasted_iota(jnp.int32, (members, LANES), 1)

    def fetch(b, half):
        return pltpu.make_async_copy(index_ref.at[b], smem[half], sems.at[half])

    for half in range(2):
        fetch(half, half).start()
    first = 0
    for part in part_refs:
        field_ref[first : first + part.shape[0]] = part[...]
        first += part.shape[0]

    def pair(i, carry):
        for half in range(2):
            b = 2 * i + half
            fetch(b, half).wait()
            for j in range(BATCH):
                acc = jnp.zeros((members, LANES), F32)
                for o in range(LANES):
                    tile = field_ref[smem[half][2 * j, o]].astype(F32)
                    acc = jnp.where(lane == o, pltpu.roll(tile, smem[half][2 * j + 1, o], 1), acc)
                out_ref[b * BATCH + j] = acc.astype(BF16)

            @pl.when(b + 2 < count)
            def _():
                fetch(b + 2, half).start()

        return carry

    lax.fori_loop(0, count // 2, pair, 0)


def observe(block, shift, fields):
    parts = [f.reshape((-1,) + f.shape[3:]) for f in fields]
    members = parts[0].shape[1]
    index = jnp.stack([block.reshape(-1, LANES), shift.reshape(-1, LANES)], 1).reshape(-1, 2 * BATCH, LANES)
    return pl.pallas_call(
        observe_kernel,
        out_shape=jax.ShapeDtypeStruct((block.shape[0] // LANES, members, LANES), BF16),
        in_specs=[VMEM] + [VMEM] * len(parts),
        out_specs=VMEM,
        scratch_shapes=[
            pltpu.VMEM((sum(p.shape[0] for p in parts), members, LANES), BF16),
            pltpu.SMEM((2 * BATCH, LANES), jnp.int32),
            pltpu.SMEM((2 * BATCH, LANES), jnp.int32),
            pltpu.SemaphoreType.DMA((2,)),
        ],
        compiler_params=params(32),
        name="observe",
    )(index, *parts)


def eye4():
    row = lax.broadcasted_iota(jnp.int32, (64, 256), 0)
    lane = lax.broadcasted_iota(jnp.int32, (64, 256), 1)
    return jnp.where(row == lane % 64, 1.0, 0.0).astype(F32)


def block_diag(x, low):
    left, right = x[:, :128], x[:, 128:]
    none = jnp.zeros_like(left)
    first, third = left * low, right * low
    top = jnp.concatenate([first, left - first, none, none], 0)
    bottom = jnp.concatenate([none, none, third, right - third], 0)
    return jnp.concatenate([top, bottom], 1)


def mul(a, b):
    return jnp.dot(a, b, preferred_element_type=F32)


LEAD = 120
GROUPS = 4


def gather_rows(q, lists_ref, cat_ref, rows_ref):
    for l in range(LANES):
        for r in range(2):
            rows_ref[q % 2, r, pl.ds(l, 1), :] = cat_ref[pl.ds(lists_ref[2 * q + r, l], 1), :]
        yield


def gram_pair(q, rows_ref, wgt_ref, first, work, consts):
    sq_ref, force_ref, scale_ref = work
    ident, lower, _, inflated = consts
    bounds = []
    rows = [rows_ref[q % 2, r] for r in range(2)]
    weighted = [(rows[r].T[:64] * wgt_ref[r, pl.ds(first + q, 1), :]).astype(BF16) for r in range(2)]
    yield
    grams = [mul(weighted[r], rows[r].astype(BF16)) for r in range(2)]
    yield
    for both in grams:
        total = jnp.sum(jnp.where(lower, jnp.abs(both), 0.0), axis=0, keepdims=True)
        bounds.append(inflated + jnp.max(total, axis=1, keepdims=True))
    turned = [pltpu.roll(x, 64, 1) for x in grams]
    inv = 1.0 / jnp.where(lower[:1], bounds[0], bounds[1])
    gram = jnp.where(lower, grams[0], turned[1])
    force = jnp.where(lower, turned[0], grams[1])
    sl = slice(q % 2 * 128, q % 2 * 128 + 128)
    sq_ref[q // 2, :, sl] = (gram + inflated * ident[:, :128]) * inv
    force_ref[q // 2, :, sl] = force.astype(BF16)
    scale_ref[q // 2, :, sl] = jnp.broadcast_to(inv, (8, 128))


def solve_stage(u, stage, held, work, consts, out_ref, first, members):
    state_ref, factor_ref = held
    sq_ref, force_ref, scale_ref = work
    ident, _, low, _ = consts
    last = 2 * NS_ITERS
    if stage == 0:
        h = (1.5 - SHIFT) * ident - 0.5 * sq_ref[u]
        product = mul(sq_ref[u].astype(BF16), block_diag(h.astype(BF16), low))
        yield
        state_ref[u, 64:] = SHIFT * ident + (1.5 - SHIFT) * ident - 0.5 * sq_ref[u]
        state_ref[u, :64] = SHIFT * sq_ref[u] + product
    elif stage < last - 1 and stage % 2 == 1:
        square = mul(state_ref[u, 64:].astype(BF16), block_diag(state_ref[u, :64].astype(BF16), low))
        yield
        factor_ref[u] = ((1.5 - SHIFT) * ident - 0.5 * square).astype(BF16)
    elif stage < last - 1:
        sl = slice(0 if stage < last - 2 else 64, 128)
        product = mul(state_ref[u, sl].astype(BF16), block_diag(factor_ref[u], low))
        yield
        state_ref[u, sl] = SHIFT * state_ref[u, sl] + product
    elif stage == last - 1:
        product = mul(state_ref[u, 64:].astype(BF16), block_diag(force_ref[u], low))
        yield
        factor_ref[u] = product.astype(BF16)
    else:
        shift = mul(state_ref[u, 64:].astype(BF16), block_diag(factor_ref[u], low))
        yield
        scale = scale_ref[u, :1]
        out_ref[first + u] = (math.sqrt(members - 1.0) * jnp.sqrt(scale)) * state_ref[u, 64:] + scale * shift


def run(steps, filler, share):
    for unit in steps:
        next(unit, None)
        for _ in range(share):
            next(filler, None)


def segment(units, gram, filler):
    middle = len(units) // 2
    begin = [gram] + units[:middle] + [gram] + units[middle:]
    run(begin, filler, LEAD // len(begin))
    run(units + [gram], filler, (LANES - LEAD) // (len(units) + 1) + 1)
    for _ in filler:
        pass


def transform_kernel(slot_ref, ens_ref, obs_ref, wgt_ref, lists_ref, out_ref, cat_ref, rows_ref, *scratch):
    work, (lists_a, lists_b, sems), held = (scratch[:3], scratch[3:6]), scratch[6:9], scratch[9:]
    smem = (lists_a, lists_b)
    groups = slot_ref.shape[0]
    _, windows, blocks, per, _ = ens_ref.shape
    members = groups * per
    count = lists_ref.shape[0]
    inflated = (members - 1) / INFL

    def fetch(b, half):
        return pltpu.make_async_copy(lists_ref.at[b], smem[half], sems.at[half])

    for half in range(2):
        fetch(half, half).start()

    def catalog(i, carry):
        w, b = i // blocks, i % blocks
        ens = jnp.concatenate([ens_ref[slot_ref[j], w, b].astype(F32) for j in range(groups)], 0)
        mean = jnp.sum(ens, axis=0, keepdims=True) * (1.0 / members)
        value = obs_ref[w, 0, pl.ds(b, 1), :]
        root = jnp.sqrt(obs_ref[w, 1, pl.ds(b, 1), :])
        anomaly = (ens - mean) * root
        innovation = jnp.broadcast_to((value - mean) * root, ens.shape)
        cat_ref[pl.ds(pl.multiple_of(i * LANES, LANES), LANES), :] = jnp.concatenate([anomaly, innovation], 0).T
        return carry

    lax.fori_loop(0, windows * blocks, catalog, 0, unroll=4)

    lower = lax.broadcasted_iota(jnp.int32, (64, 128), 1) < 64
    consts = (eye4(), lower, jnp.where(lower, 1.0, 0.0).astype(BF16), inflated)
    pairs = 2 * GROUPS
    last = 2 * NS_ITERS

    def solve(stage, block, half):
        at = jnp.maximum(block, 0) * GROUPS
        return [solve_stage(u, stage, held, work[half], consts, out_ref, at, members) for u in range(GROUPS)]

    def gram(q, block, half):
        return gram_pair(q, rows_ref, wgt_ref, jnp.maximum(block, 0) * pairs, work[half], consts)

    def step(i, carry):
        for half in range(2):
            b = 2 * i + half
            for q in range(pairs):

                @pl.when(slot_ref[0] >= 0)
                def _():
                    if q == 0:
                        fetch(b, half).wait()
                        units = solve(last - 1, b - 2, half)
                        before = gram(pairs - 1, b - 1, 1 - half)
                    else:
                        units = solve(last, b - 2, half) if q == 1 else []
                        units += solve(q - 1, b - 1, 1 - half)
                        before = gram(q - 1, b, half)
                    segment(units, before, gather_rows(q, smem[half], cat_ref, rows_ref))

            @pl.when(b + 2 < count)
            def _():
                fetch(b + 2, half).start()

        return carry

    lax.fori_loop(0, count // 2, step, 0)
    def finish(units):
        for _ in range(3):
            run(units, iter(()), 0)

    for stage in (last - 1, last):
        finish(solve(stage, count - 2, 0))
    finish([gram(pairs - 1, count - 1, 1)])
    for stage in range(last + 1):
        finish(solve(stage, count - 1, 1))


def transforms(slots, lists, ens, obs, wgt):
    columns = lists.shape[1]
    pairs = columns // 2
    _, windows, blocks, _, _ = ens.shape
    lists = lists.reshape(2, pairs // GROUPS, 2 * GROUPS, LANES).transpose(1, 2, 0, 3).reshape(-1, 4 * GROUPS, LANES)
    work = [
        pltpu.VMEM((GROUPS, 64, 256), F32),
        pltpu.VMEM((GROUPS, 64, 256), BF16),
        pltpu.VMEM((GROUPS, 8, 256), F32),
    ]
    return pl.pallas_call(
        transform_kernel,
        out_shape=jax.ShapeDtypeStruct((pairs, 64, 256), F32),
        in_specs=[SMEM] + [VMEM] * 4,
        out_specs=VMEM,
        scratch_shapes=[
            pltpu.VMEM((windows * blocks * LANES, LANES), F32),
            pltpu.VMEM((2, 2, LANES, LANES), F32),
            *work,
            *work,
            pltpu.SMEM((4 * GROUPS, LANES), jnp.int32),
            pltpu.SMEM((4 * GROUPS, LANES), jnp.int32),
            pltpu.SemaphoreType.DMA((2,)),
            pltpu.VMEM((GROUPS, 128, 256), F32),
            pltpu.VMEM((GROUPS, 64, 256), BF16),
        ],
        compiler_params=params(48),
        name="transforms",
    )(slots, ens, obs, wgt, lists)


def update_kernel(state_ref, transform_ref, out_ref, cells_ref, moved_ref, center_ref):
    groups, levels, _, tiles, per, _ = state_ref.shape
    width = tiles * LANES
    members = groups * per
    pairs = transform_ref.shape[0]

    def enter(z, carry):
        parts = []
        for r in range(2):
            blocks = [[state_ref[j, z, r, t].astype(F32) for j in range(groups)] for t in range(tiles)]
            state = jnp.concatenate([jnp.concatenate(b, 0) for b in blocks], 1)
            center = jnp.sum(state, axis=0, keepdims=True) * (1.0 / members)
            center_ref[z, pl.ds(r, 1), :] = center
            parts.append(state - center)
        cells_ref[pl.ds(pl.multiple_of(z * width, width), width), :] = jnp.concatenate(parts, 0).T
        return carry

    lax.fori_loop(0, levels, enter, 0, unroll=4)

    ident = eye4()
    lane = lax.broadcasted_iota(jnp.int32, (64, 128), 1)
    low = jnp.where(lane < 64, 1.0, 0.0).astype(BF16)

    def apply(g, carry):
        halves = []
        for half in range(2):
            q = g * 2 + half
            halves.append(jnp.concatenate([cells_ref[pl.ds(2 * q + c, levels, stride=width), :] for c in range(2)], 0))
        x = jnp.concatenate(halves, 1)
        t = transform_ref[g]
        on = t * ident
        diag = jnp.sum(on, axis=0, keepdims=True)
        y = x * diag + mul(x.astype(BF16), block_diag((t - on).astype(BF16), low))
        for half in range(2):
            q = g * 2 + half
            for c in range(2):
                moved_ref[pl.ds(2 * q + c, levels, stride=width), :] = y[c * levels : (c + 1) * levels, half * 128 : half * 128 + 128]
        return carry

    lax.fori_loop(0, pairs, apply, 0, unroll=4)

    def leave(z, carry):
        back = moved_ref[pl.ds(pl.multiple_of(z * width, width), width), :].T
        for r in range(2):
            out_ref[z, r] = (back[r * members : (r + 1) * members] + center_ref[z, pl.ds(r, 1), :]).astype(BF16)
        return carry

    lax.fori_loop(0, levels, leave, 0, unroll=4)


def update(state, transform):
    groups, levels, rows, tiles, per, _ = state.shape
    width = tiles * LANES
    return pl.pallas_call(
        update_kernel,
        out_shape=jax.ShapeDtypeStruct((levels, rows, groups * per, width), BF16),
        in_specs=[VMEM, VMEM],
        out_specs=VMEM,
        scratch_shapes=[
            pltpu.VMEM((levels * width, LANES), F32),
            pltpu.VMEM((levels * width, LANES), F32),
            pltpu.VMEM((levels, 8, width), F32),
        ],
        compiler_params=params(48),
        name="update",
    )(state, transform)


def cuts(levels):
    eighth = levels // 8
    ends = [0, eighth, 3 * eighth, 5 * eighth, 7 * eighth, levels]
    return list(zip(ends[:-1], ends[1:]))


def bit_reversed(value, bits):
    return sum(((value >> b) & 1) << (bits - 1 - b) for b in range(bits))


def on_device(prior, coefficients, measured, precision, location, lists, counts, loc_weight):
    slabs = lax.axis_size("slab")
    groups = lax.axis_size("mem")
    bits = groups.bit_length() - 1
    me = lax.axis_index("mem")
    up = [(i, i + 1) for i in range(slabs - 1)]
    down = [(i + 1, i) for i in range(slabs - 1)]
    swap = [(i, i ^ 1) for i in range(slabs)]
    skip = [(i, i + 2) for i in range(0, slabs - 2, 2)] + [(i, i - 2) for i in range(3, slabs, 2)]
    odd = lax.axis_index("slab") % 2 == 1
    columns = prior.shape[3]
    nobs = measured.shape[0]

    levels, members = prior.shape[1], prior.shape[0]
    own = jnp.transpose(prior, (1, 2, 0, 3))
    coef = jnp.transpose(coefficients, (0, 2, 1, 3))
    spans = cuts(levels)
    pieces = [own[first:last].reshape(-1, members, columns) for first, last in spans]
    extra = coef.astype(BF16).reshape(-1, members, columns)
    pieces[0] = jnp.concatenate([pieces[0], extra], 0)
    pieces = lax.optimization_barrier(pieces)
    flag = odd.astype(jnp.int32).reshape(1)
    besides, beyonds, fields = [], [], []

    def advance_piece(i):
        nonlocal cprev, cnext
        if i == 0:
            sides = [x[0][-extra.shape[0] :].reshape(coef.shape).astype(F32) for x in (besides, beyonds)]
            cprev = jnp.where(odd, sides[0][:, 1], sides[1][:, 1])
            cnext = jnp.where(odd, sides[1][:, 0], sides[0][:, 0])
        fields.append(forecast(spans[i], flag, pieces[i], besides[i], beyonds[i], coef, cprev, cnext))

    cprev = cnext = None
    for i, piece in enumerate(pieces):
        if i >= 3:
            advance_piece(i - 3)
            fields[i - 3], piece = lax.optimization_barrier((fields[i - 3], piece))
        besides.append(lax.ppermute(piece, "slab", swap))
        if i >= 2:
            beyonds.append(lax.ppermute(besides[i - 2], "slab", skip))
    beyonds += [lax.ppermute(beside, "slab", skip) for beside in besides[-2:]]
    for i in range(len(fields), len(pieces)):
        advance_piece(i)

    zr, col = location // columns, location % columns
    block = zr * (columns // LANES) + col // LANES
    shift = (jnp.arange(nobs, dtype=jnp.int32) - col) % LANES
    seen = observe(block, shift, fields)
    extras = jnp.stack([measured, precision], 0)
    high = extras.astype(BF16)
    extras = jnp.concatenate([high, (extras - high.astype(F32)).astype(BF16)], 0)
    sent = jnp.concatenate([seen, extras.reshape((-1,) + seen.shape[1:])], 0)
    window = jnp.stack([lax.ppermute(sent, "slab", up), sent, lax.ppermute(sent, "slab", down)], 0)
    obs = window[:, seen.shape[0] :].reshape(3, 2, 2, nobs // LANES, LANES).astype(F32)
    obs = obs[:, 0] + obs[:, 1]
    window = window[:, : seen.shape[0]]
    ens = window[None]
    step = groups // 2
    while step:
        ens = jnp.concatenate([ens, lax.ppermute(ens, "mem", [(i, i ^ step) for i in range(groups)])], 0)
        step //= 2
    slots = bit_reversed(jnp.arange(groups, dtype=jnp.int32) ^ me, bits)

    position = lax.broadcasted_iota(jnp.int32, loc_weight.shape, 2)
    wgt = jnp.where(position < counts[..., None], loc_weight, 0.0)
    transform = transforms(slots, lists, ens, obs, wgt)

    tiles = columns // groups // LANES
    ship = jnp.concatenate(fields, 0)
    ship = ship.reshape(ship.shape[:2] + (groups, tiles) + ship.shape[3:])
    ship, _ = lax.optimization_barrier((jnp.transpose(ship, (2, 0, 1, 3, 4, 5)), ens))
    state = lax.all_to_all(ship, "mem", 0, 0, tiled=False)
    result = update(state, transform)
    return jnp.transpose(result, (2, 0, 1, 3))


def solution(mesh):
    return jax.shard_map(
        on_device,
        mesh=mesh,
        in_specs=(
            P("mem", None, "slab", None),
            P(None, None, "slab", None),
            P("slab"),
            P("slab"),
            P("slab"),
            P("slab", "mem", None),
            P("slab", "mem"),
            P("slab", "mem", None),
        ),
        out_specs=P(None, None, "slab", "mem"),
        check_vma=False,
    )
```

```python
import functools
import itertools
import math

import jax
import jax.numpy as jnp
from jax import lax
from jax.experimental import pallas as pl
from jax.experimental.pallas import tpu as pltpu
from jax.sharding import PartitionSpec as P

NS_ITERS = 4
INFL = 1.1
SHIFT = 1.25
LANES = 128
F32 = jnp.float32
BF16 = jnp.bfloat16
VMEM = pl.BlockSpec(memory_space=pltpu.VMEM)
SMEM = pl.BlockSpec(memory_space=pltpu.SMEM)


def params(mib):
    return pltpu.CompilerParams(vmem_limit_bytes=mib * 1024 * 1024)


def advance(upper, lower, center, c):
    width = center.shape[1]
    east = pltpu.roll(center, width - 1, 1)
    west = pltpu.roll(center, 1, 1)
    advect = c[0] * (upper - lower) + c[1] * (east - west)
    laplace = upper + lower + east + west - 4.0 * center
    return center - 0.5 * advect + c[2] * laplace


def forecast_kernel(first, odd_ref, own_ref, beside_ref, beyond_ref, coef_ref, cprev_ref, cnext_ref, field_ref):
    levels, width = field_ref.shape[0], own_ref.shape[2]
    odd = odd_ref[0] == 1

    def level(z, carry):
        beside = [beside_ref[2 * z + r].astype(F32) for r in range(2)]
        beyond = [beyond_ref[2 * z + r].astype(F32) for r in range(2)]
        rows = [jnp.where(odd, beside[r], beyond[r]) for r in range(2)]
        rows += [own_ref[2 * z + r].astype(F32) for r in range(2)]
        rows += [jnp.where(odd, beyond[r], beside[r]) for r in range(2)]
        at = pl.ds(first + z, 1)
        coeffs = [
            [cprev_ref[k, at, :] for k in range(3)],
            [coef_ref[k, 0, at, :] for k in range(3)],
            [coef_ref[k, 1, at, :] for k in range(3)],
            [cnext_ref[k, at, :] for k in range(3)],
        ]
        once = [advance(rows[i + 2], rows[i], rows[i + 1], coeffs[i]) for i in range(4)]
        for r in range(2):
            twice = advance(once[r + 2], once[r], once[r + 1], coeffs[r + 1]).astype(BF16)
            for t in range(width // LANES):
                field_ref[z, r, t] = twice[:, t * LANES : (t + 1) * LANES]
        return carry

    lax.fori_loop(0, levels, level, 0)


def forecast(span, odd, own, beside, beyond, coef, cprev, cnext):
    first, levels, rows = span[0], span[1] - span[0], coef.shape[1]
    _, members, width = own.shape
    return pl.pallas_call(
        functools.partial(forecast_kernel, first),
        out_shape=jax.ShapeDtypeStruct((levels, rows, width // LANES, members, LANES), BF16),
        in_specs=[SMEM] + [VMEM] * 6,
        out_specs=VMEM,
        compiler_params=params(32),
        name="forecast",
    )(odd, own, beside, beyond, coef, cprev, cnext)


BATCH = 4


def observe_kernel(index_ref, *refs):
    *part_refs, out_ref, field_ref, smem_a, smem_b, sems = refs
    smem = (smem_a, smem_b)
    count = index_ref.shape[0]
    members = out_ref.shape[1]
    lane = lax.broadcasted_iota(jnp.int32, (members, LANES), 1)

    def fetch(b, half):
        return pltpu.make_async_copy(index_ref.at[b], smem[half], sems.at[half])

    for half in range(2):
        fetch(half, half).start()
    first = 0
    for part in part_refs:
        field_ref[first : first + part.shape[0]] = part[...]
        first += part.shape[0]

    def pair(i, carry):
        for half in range(2):
            b = 2 * i + half
            fetch(b, half).wait()
            for j in range(BATCH):
                acc = jnp.zeros((members, LANES), F32)
                for o in range(LANES):
                    tile = field_ref[smem[half][2 * j, o]].astype(F32)
                    acc = jnp.where(lane == o, pltpu.roll(tile, smem[half][2 * j + 1, o], 1), acc)
                out_ref[b * BATCH + j] = acc.astype(BF16)

            @pl.when(b + 2 < count)
            def _():
                fetch(b + 2, half).start()

        return carry

    lax.fori_loop(0, count // 2, pair, 0)


def observe(block, shift, fields):
    parts = [f.reshape((-1,) + f.shape[3:]) for f in fields]
    members = parts[0].shape[1]
    index = jnp.stack([block.reshape(-1, LANES), shift.reshape(-1, LANES)], 1).reshape(-1, 2 * BATCH, LANES)
    return pl.pallas_call(
        observe_kernel,
        out_shape=jax.ShapeDtypeStruct((block.shape[0] // LANES, members, LANES), BF16),
        in_specs=[VMEM] + [VMEM] * len(parts),
        out_specs=VMEM,
        scratch_shapes=[
            pltpu.VMEM((sum(p.shape[0] for p in parts), members, LANES), BF16),
            pltpu.SMEM((2 * BATCH, LANES), jnp.int32),
            pltpu.SMEM((2 * BATCH, LANES), jnp.int32),
            pltpu.SemaphoreType.DMA((2,)),
        ],
        compiler_params=params(32),
        name="observe",
    )(index, *parts)


def eye4():
    row = lax.broadcasted_iota(jnp.int32, (64, 256), 0)
    lane = lax.broadcasted_iota(jnp.int32, (64, 256), 1)
    return jnp.where(row == lane % 64, 1.0, 0.0).astype(F32)


def block_diag(x, low):
    left, right = x[:, :128], x[:, 128:]
    none = jnp.zeros_like(left)
    first, third = left * low, right * low
    top = jnp.concatenate([first, left - first, none, none], 0)
    bottom = jnp.concatenate([none, none, third, right - third], 0)
    return jnp.concatenate([top, bottom], 1)


def mul(a, b):
    return jnp.dot(a, b, preferred_element_type=F32)


WIDE = 2
LEAD = 236
GROUPS = 4


def gather_rows(q, lists_ref, cat_ref, rows_ref):
    for l in range(LANES):
        for r in range(2):
            rows_ref[q % (2 * WIDE), r, pl.ds(l, 1), :] = cat_ref[pl.ds(lists_ref[2 * q + r, l], 1), :]
        yield


def gram_pair(q, rows_ref, wgt_ref, first, work, consts):
    sq_ref, force_ref, scale_ref = work
    ident, lower, _, inflated = consts
    bounds = []
    rows = [rows_ref[q % (2 * WIDE), r] for r in range(2)]
    weighted = [(rows[r].T[:64] * wgt_ref[r, pl.ds(first + q, 1), :]).astype(BF16) for r in range(2)]
    yield
    grams = [mul(weighted[r], rows[r].astype(BF16)) for r in range(2)]
    yield
    for both in grams:
        total = jnp.sum(jnp.where(lower, jnp.abs(both), 0.0), axis=0, keepdims=True)
        bounds.append(inflated + jnp.max(total, axis=1, keepdims=True))
    turned = [pltpu.roll(x, 64, 1) for x in grams]
    inv = 1.0 / jnp.where(lower[:1], bounds[0], bounds[1])
    gram = jnp.where(lower, grams[0], turned[1])
    force = jnp.where(lower, turned[0], grams[1])
    sl = slice(q % 2 * 128, q % 2 * 128 + 128)
    sq_ref[q // 2, :, sl] = (gram + inflated * ident[:, :128]) * inv
    force_ref[q // 2, :, sl] = force.astype(BF16)
    scale_ref[q // 2, :, sl] = jnp.broadcast_to(inv, (8, 128))


def solve_stage(u, stage, held, work, consts, out_ref, first, members):
    state_ref, factor_ref = held
    sq_ref, force_ref, scale_ref = work
    ident, _, low, _ = consts
    last = 2 * NS_ITERS
    if stage == 0:
        h = (1.5 - SHIFT) * ident - 0.5 * sq_ref[u]
        product = mul(sq_ref[u].astype(BF16), block_diag(h.astype(BF16), low))
        yield
        state_ref[u, 64:] = SHIFT * ident + (1.5 - SHIFT) * ident - 0.5 * sq_ref[u]
        state_ref[u, :64] = SHIFT * sq_ref[u] + product
    elif stage < last - 1 and stage % 2 == 1:
        square = mul(state_ref[u, 64:].astype(BF16), block_diag(state_ref[u, :64].astype(BF16), low))
        yield
        factor_ref[u] = ((1.5 - SHIFT) * ident - 0.5 * square).astype(BF16)
    elif stage < last - 1:
        sl = slice(0 if stage < last - 2 else 64, 128)
        product = mul(state_ref[u, sl].astype(BF16), block_diag(factor_ref[u], low))
        yield
        state_ref[u, sl] = SHIFT * state_ref[u, sl] + product
    elif stage == last - 1:
        product = mul(state_ref[u, 64:].astype(BF16), block_diag(force_ref[u], low))
        yield
        factor_ref[u] = product.astype(BF16)
    else:
        shift = mul(state_ref[u, 64:].astype(BF16), block_diag(factor_ref[u], low))
        yield
        scale = scale_ref[u, :1]
        out_ref[first + u] = (math.sqrt(members - 1.0) * jnp.sqrt(scale)) * state_ref[u, 64:] + scale * shift


def run(steps, filler, share):
    for unit in steps:
        next(unit, None)
        for _ in range(share):
            next(filler, None)


def segment(stages, grams, filler):
    steps = grams + stages[0] + grams
    for i, (before, after) in enumerate(zip(stages[:-1], stages[1:])):
        for pair in zip(before, after):
            steps += pair
        if i == 0:
            steps += grams
    run(steps, filler, LEAD // len(steps))
    run(stages[-1], filler, (WIDE * LANES - LEAD) // len(stages[-1]) + 1)
    for _ in filler:
        pass


def transform_kernel(slot_ref, ens_ref, obs_ref, wgt_ref, lists_ref, out_ref, cat_ref, rows_ref, *scratch):
    work, (lists_a, lists_b, sems), held = (scratch[:3], scratch[3:6]), scratch[6:9], scratch[9:]
    smem = (lists_a, lists_b)
    groups = slot_ref.shape[0]
    _, windows, blocks, per, _ = ens_ref.shape
    members = groups * per
    count = lists_ref.shape[0]
    inflated = (members - 1) / INFL

    def fetch(b, half):
        return pltpu.make_async_copy(lists_ref.at[b], smem[half], sems.at[half])

    for half in range(2):
        fetch(half, half).start()

    def catalog(i, carry):
        w, b = i // blocks, i % blocks
        ens = jnp.concatenate([ens_ref[slot_ref[j], w, b].astype(F32) for j in range(groups)], 0)
        mean = jnp.sum(ens, axis=0, keepdims=True) * (1.0 / members)
        value = obs_ref[w, 0, pl.ds(b, 1), :]
        root = jnp.sqrt(obs_ref[w, 1, pl.ds(b, 1), :])
        anomaly = (ens - mean) * root
        innovation = jnp.broadcast_to((value - mean) * root, ens.shape)
        cat_ref[pl.ds(pl.multiple_of(i * LANES, LANES), LANES), :] = jnp.concatenate([anomaly, innovation], 0).T
        return carry

    lax.fori_loop(0, windows * blocks, catalog, 0, unroll=4)

    lower = lax.broadcasted_iota(jnp.int32, (64, 128), 1) < 64
    consts = (eye4(), lower, jnp.where(lower, 1.0, 0.0).astype(BF16), inflated)
    pairs = 2 * GROUPS
    last = 2 * NS_ITERS
    share = (last + 1) * WIDE // pairs

    def solve(stage, block, half):
        at = jnp.maximum(block, 0) * GROUPS
        return [solve_stage(u, stage, held, work[half], consts, out_ref, at, members) for u in range(GROUPS)]

    def gram(q, block, half):
        return gram_pair(q, rows_ref, wgt_ref, jnp.maximum(block, 0) * pairs, work[half], consts)

    def step(i, carry):
        for half in range(2):
            b = 2 * i + half
            for part in range(pairs // WIDE):

                @pl.when(slot_ref[0] >= 0)
                def _():
                    if part == 0:
                        fetch(b, half).wait()
                        stages = [solve(stage, b - 2, half) for stage in range(pairs // WIDE * share - share, last + 1)]
                        grams = [gram(q, b - 1, 1 - half) for q in range(pairs - WIDE, pairs)]
                    else:
                        stages = [solve(stage, b - 1, 1 - half) for stage in range(part * share - share, part * share)]
                        grams = [gram(q, b, half) for q in range((part - 1) * WIDE, part * WIDE)]
                    rows = [gather_rows(q, smem[half], cat_ref, rows_ref) for q in range(part * WIDE, (part + 1) * WIDE)]
                    segment(stages, grams, itertools.chain(*rows))

            @pl.when(b + 2 < count)
            def _():
                fetch(b + 2, half).start()

        return carry

    lax.fori_loop(0, count // 2, step, 0)

    def finish(units):
        for _ in range(3):
            run(units, iter(()), 0)

    for stage in range(pairs // WIDE * share - share, last + 1):
        finish(solve(stage, count - 2, 0))
    finish([gram(q, count - 1, 1) for q in range(pairs - WIDE, pairs)])
    for stage in range(last + 1):
        finish(solve(stage, count - 1, 1))


def transforms(slots, lists, ens, obs, wgt):
    columns = lists.shape[1]
    pairs = columns // 2
    _, windows, blocks, _, _ = ens.shape
    lists = lists.reshape(2, pairs // GROUPS, 2 * GROUPS, LANES).transpose(1, 2, 0, 3).reshape(-1, 4 * GROUPS, LANES)
    work = [
        pltpu.VMEM((GROUPS, 64, 256), F32),
        pltpu.VMEM((GROUPS, 64, 256), BF16),
        pltpu.VMEM((GROUPS, 8, 256), F32),
    ]
    return pl.pallas_call(
        transform_kernel,
        out_shape=jax.ShapeDtypeStruct((pairs, 64, 256), F32),
        in_specs=[SMEM] + [VMEM] * 4,
        out_specs=VMEM,
        scratch_shapes=[
            pltpu.VMEM((windows * blocks * LANES, LANES), F32),
            pltpu.VMEM((2 * WIDE, 2, LANES, LANES), F32),
            *work,
            *work,
            pltpu.SMEM((4 * GROUPS, LANES), jnp.int32),
            pltpu.SMEM((4 * GROUPS, LANES), jnp.int32),
            pltpu.SemaphoreType.DMA((2,)),
            pltpu.VMEM((GROUPS, 128, 256), F32),
            pltpu.VMEM((GROUPS, 64, 256), BF16),
        ],
        compiler_params=params(24),
        name="transforms",
    )(slots, ens, obs, wgt, lists)


def update_kernel(state_ref, transform_ref, out_ref, cells_ref, moved_ref, center_ref):
    groups, levels, _, tiles, per, _ = state_ref.shape
    width = tiles * LANES
    members = groups * per
    pairs = transform_ref.shape[0]

    def enter(z, carry):
        parts = []
        for r in range(2):
            blocks = [[state_ref[j, z, r, t].astype(F32) for j in range(groups)] for t in range(tiles)]
            state = jnp.concatenate([jnp.concatenate(b, 0) for b in blocks], 1)
            center = jnp.sum(state, axis=0, keepdims=True) * (1.0 / members)
            center_ref[z, pl.ds(r, 1), :] = center
            parts.append(state - center)
        cells_ref[pl.ds(pl.multiple_of(z * width, width), width), :] = jnp.concatenate(parts, 0).T
        return carry

    lax.fori_loop(0, levels, enter, 0, unroll=4)

    ident = eye4()
    lane = lax.broadcasted_iota(jnp.int32, (64, 128), 1)
    low = jnp.where(lane < 64, 1.0, 0.0).astype(BF16)

    def apply(g, carry):
        halves = []
        for half in range(2):
            q = g * 2 + half
            halves.append(jnp.concatenate([cells_ref[pl.ds(2 * q + c, levels, stride=width), :] for c in range(2)], 0))
        x = jnp.concatenate(halves, 1)
        t = transform_ref[g]
        on = t * ident
        diag = jnp.sum(on, axis=0, keepdims=True)
        y = x * diag + mul(x.astype(BF16), block_diag((t - on).astype(BF16), low))
        for half in range(2):
            q = g * 2 + half
            for c in range(2):
                moved_ref[pl.ds(2 * q + c, levels, stride=width), :] = y[c * levels : (c + 1) * levels, half * 128 : half * 128 + 128]
        return carry

    lax.fori_loop(0, pairs, apply, 0, unroll=4)

    def leave(z, carry):
        back = moved_ref[pl.ds(pl.multiple_of(z * width, width), width), :].T
        for r in range(2):
            out_ref[z, r] = (back[r * members : (r + 1) * members] + center_ref[z, pl.ds(r, 1), :]).astype(BF16)
        return carry

    lax.fori_loop(0, levels, leave, 0, unroll=4)


def update(state, transform):
    groups, levels, rows, tiles, per, _ = state.shape
    width = tiles * LANES
    return pl.pallas_call(
        update_kernel,
        out_shape=jax.ShapeDtypeStruct((levels, rows, groups * per, width), BF16),
        in_specs=[VMEM, VMEM],
        out_specs=VMEM,
        scratch_shapes=[
            pltpu.VMEM((levels * width, LANES), F32),
            pltpu.VMEM((levels * width, LANES), F32),
            pltpu.VMEM((levels, 8, width), F32),
        ],
        compiler_params=params(24),
        name="update",
    )(state, transform)


def cuts(levels):
    eighth = levels // 8
    ends = [0, eighth, 3 * eighth, 5 * eighth, 7 * eighth, levels]
    return list(zip(ends[:-1], ends[1:]))


def bit_reversed(value, bits):
    return sum(((value >> b) & 1) << (bits - 1 - b) for b in range(bits))


def on_device(prior, coefficients, measured, precision, location, lists, counts, loc_weight):
    slabs = lax.axis_size("slab")
    groups = lax.axis_size("mem")
    bits = groups.bit_length() - 1
    me = lax.axis_index("mem")
    up = [(i, i + 1) for i in range(slabs - 1)]
    down = [(i + 1, i) for i in range(slabs - 1)]
    swap = [(i, i ^ 1) for i in range(slabs)]
    skip = [(i, i + 2) for i in range(0, slabs - 2, 2)] + [(i, i - 2) for i in range(3, slabs, 2)]
    odd = lax.axis_index("slab") % 2 == 1
    columns = prior.shape[3]
    nobs = measured.shape[0]

    levels, members = prior.shape[1], prior.shape[0]
    own = jnp.transpose(prior, (1, 2, 0, 3))
    coef = jnp.transpose(coefficients, (0, 2, 1, 3))
    spans = cuts(levels)
    pieces = [own[first:last].reshape(-1, members, columns) for first, last in spans]
    extra = coef.astype(BF16).reshape(-1, members, columns)
    pieces[0] = jnp.concatenate([pieces[0], extra], 0)
    pieces = lax.optimization_barrier(pieces)
    flag = odd.astype(jnp.int32).reshape(1)
    besides, beyonds, fields = [], [], []

    def advance_piece(i):
        nonlocal cprev, cnext
        if i == 0:
            sides = [x[0][-extra.shape[0] :].reshape(coef.shape).astype(F32) for x in (besides, beyonds)]
            cprev = jnp.where(odd, sides[0][:, 1], sides[1][:, 1])
            cnext = jnp.where(odd, sides[1][:, 0], sides[0][:, 0])
        fields.append(forecast(spans[i], flag, pieces[i], besides[i], beyonds[i], coef, cprev, cnext))

    cprev = cnext = None
    for i, piece in enumerate(pieces):
        if i >= 3:
            advance_piece(i - 3)
            fields[i - 3], piece = lax.optimization_barrier((fields[i - 3], piece))
        besides.append(lax.ppermute(piece, "slab", swap))
        if i >= 2:
            beyonds.append(lax.ppermute(besides[i - 2], "slab", skip))
    beyonds += [lax.ppermute(beside, "slab", skip) for beside in besides[-2:]]
    for i in range(len(fields), len(pieces)):
        advance_piece(i)

    zr, col = location // columns, location % columns
    block = zr * (columns // LANES) + col // LANES
    shift = (jnp.arange(nobs, dtype=jnp.int32) - col) % LANES
    seen = observe(block, shift, fields)
    extras = jnp.stack([measured, precision], 0)
    high = extras.astype(BF16)
    extras = jnp.concatenate([high, (extras - high.astype(F32)).astype(BF16)], 0)
    sent = jnp.concatenate([seen, extras.reshape((-1,) + seen.shape[1:])], 0)
    window = jnp.stack([lax.ppermute(sent, "slab", up), sent, lax.ppermute(sent, "slab", down)], 0)
    obs = window[:, seen.shape[0] :].reshape(3, 2, 2, nobs // LANES, LANES).astype(F32)
    obs = obs[:, 0] + obs[:, 1]
    window = window[:, : seen.shape[0]]
    tiles = columns // groups // LANES
    ship = jnp.concatenate(fields, 0)
    ship = jnp.transpose(ship.reshape(ship.shape[:2] + (groups, tiles) + ship.shape[3:]), (2, 0, 1, 3, 4, 5))
    ens = window[None]
    distance = groups // 2
    while distance:
        ens = jnp.concatenate([ens, lax.ppermute(ens, "mem", [(i, i ^ distance) for i in range(groups)])], 0)
        if distance == groups // 2:
            ens, ship = lax.optimization_barrier((ens, ship))
        distance //= 2
    slots = bit_reversed(jnp.arange(groups, dtype=jnp.int32) ^ me, bits)

    position = lax.broadcasted_iota(jnp.int32, loc_weight.shape, 2)
    wgt = jnp.where(position < counts[..., None], loc_weight, 0.0)
    transform = transforms(slots, lists, ens, obs, wgt)

    ship, _ = lax.optimization_barrier((ship, ens))
    state = lax.all_to_all(ship, "mem", 0, 0, tiled=False)
    result = update(state, transform)
    return jnp.transpose(result, (2, 0, 1, 3))


def solution(mesh):
    return jax.shard_map(
        on_device,
        mesh=mesh,
        in_specs=(
            P("mem", None, "slab", None),
            P(None, None, "slab", None),
            P("slab"),
            P("slab"),
            P("slab"),
            P("slab", "mem", None),
            P("slab", "mem"),
            P("slab", "mem", None),
        ),
        out_specs=P(None, None, "slab", "mem"),
        check_vma=False,
    )
```

```python
import functools
import itertools
import math

import jax
import jax.numpy as jnp
from jax import lax
from jax.experimental import pallas as pl
from jax.experimental.pallas import tpu as pltpu
from jax.sharding import PartitionSpec as P

NS_ITERS = 4
INFL = 1.1
SHIFT = 1.25
LANES = 128
F32 = jnp.float32
BF16 = jnp.bfloat16
VMEM = pl.BlockSpec(memory_space=pltpu.VMEM)
SMEM = pl.BlockSpec(memory_space=pltpu.SMEM)


def params(mib):
    return pltpu.CompilerParams(vmem_limit_bytes=mib * 1024 * 1024)


def advance(upper, lower, center, c):
    width = center.shape[1]
    east = pltpu.roll(center, width - 1, 1)
    west = pltpu.roll(center, 1, 1)
    advect = c[0] * (upper - lower) + c[1] * (east - west)
    laplace = upper + lower + east + west - 4.0 * center
    return center - 0.5 * advect + c[2] * laplace


def forecast_kernel(first, odd_ref, own_ref, beside_ref, beyond_ref, coef_ref, cprev_ref, cnext_ref, field_ref):
    levels, width = field_ref.shape[0], own_ref.shape[2]
    odd = odd_ref[0] == 1
    share = cprev_ref.shape[2]

    def level(z, carry):
        beside = [beside_ref[2 * z + r].astype(F32) for r in range(2)]
        beyond = [beyond_ref[2 * z + r].astype(F32) for r in range(2)]
        rows = [jnp.where(odd, beside[r], beyond[r]) for r in range(2)]
        rows += [own_ref[2 * z + r].astype(F32) for r in range(2)]
        rows += [jnp.where(odd, beyond[r], beside[r]) for r in range(2)]
        at = pl.ds(first + z, 1)
        coeffs = [
            [cprev_ref[(first + z) // share, k, pl.ds((first + z) % share, 1), :] for k in range(3)],
            [coef_ref[k, 0, at, :] for k in range(3)],
            [coef_ref[k, 1, at, :] for k in range(3)],
            [cnext_ref[(first + z) // share, k, pl.ds((first + z) % share, 1), :] for k in range(3)],
        ]
        once = [advance(rows[i + 2], rows[i], rows[i + 1], coeffs[i]) for i in range(4)]
        for r in range(2):
            twice = advance(once[r + 2], once[r], once[r + 1], coeffs[r + 1]).astype(BF16)
            for t in range(width // LANES):
                field_ref[z, r, t] = twice[:, t * LANES : (t + 1) * LANES]
        return carry

    lax.fori_loop(0, levels, level, 0)


def forecast(span, odd, own, beside, beyond, coef, cprev, cnext):
    first, levels, rows = span[0], span[1] - span[0], coef.shape[1]
    _, members, width = own.shape
    return pl.pallas_call(
        functools.partial(forecast_kernel, first),
        out_shape=jax.ShapeDtypeStruct((levels, rows, width // LANES, members, LANES), BF16),
        in_specs=[SMEM] + [VMEM] * 6,
        out_specs=VMEM,
        compiler_params=params(32),
        name="forecast",
    )(odd, own, beside, beyond, coef, cprev, cnext)


BATCH = 4


def observe_kernel(index_ref, *refs):
    *part_refs, out_ref, field_ref, smem_a, smem_b, sems = refs
    smem = (smem_a, smem_b)
    count = index_ref.shape[0]
    members = out_ref.shape[1]
    lane = lax.broadcasted_iota(jnp.int32, (members, LANES), 1)

    def fetch(b, half):
        return pltpu.make_async_copy(index_ref.at[b], smem[half], sems.at[half])

    for half in range(2):
        fetch(half, half).start()
    first = 0
    for part in part_refs:
        field_ref[first : first + part.shape[0]] = part[...]
        first += part.shape[0]

    def pair(i, carry):
        for half in range(2):
            b = 2 * i + half
            fetch(b, half).wait()
            for j in range(BATCH):
                acc = jnp.zeros((members, LANES), F32)
                for o in range(LANES):
                    tile = field_ref[smem[half][2 * j, o]].astype(F32)
                    acc = jnp.where(lane == o, pltpu.roll(tile, smem[half][2 * j + 1, o], 1), acc)
                out_ref[b * BATCH + j] = acc.astype(BF16)

            @pl.when(b + 2 < count)
            def _():
                fetch(b + 2, half).start()

        return carry

    lax.fori_loop(0, count // 2, pair, 0)


def observe(block, shift, fields):
    parts = [f.reshape((-1,) + f.shape[3:]) for f in fields]
    members = parts[0].shape[1]
    index = jnp.stack([block.reshape(-1, LANES), shift.reshape(-1, LANES)], 1).reshape(-1, 2 * BATCH, LANES)
    return pl.pallas_call(
        observe_kernel,
        out_shape=jax.ShapeDtypeStruct((block.shape[0] // LANES, members, LANES), BF16),
        in_specs=[VMEM] + [VMEM] * len(parts),
        out_specs=VMEM,
        scratch_shapes=[
            pltpu.VMEM((sum(p.shape[0] for p in parts), members, LANES), BF16),
            pltpu.SMEM((2 * BATCH, LANES), jnp.int32),
            pltpu.SMEM((2 * BATCH, LANES), jnp.int32),
            pltpu.SemaphoreType.DMA((2,)),
        ],
        compiler_params=params(32),
        name="observe",
    )(index, *parts)


def eye4():
    row = lax.broadcasted_iota(jnp.int32, (64, 256), 0)
    lane = lax.broadcasted_iota(jnp.int32, (64, 256), 1)
    return jnp.where(row == lane % 64, 1.0, 0.0).astype(F32)


def block_diag(x, low):
    left, right = x[:, :128], x[:, 128:]
    none = jnp.zeros_like(left)
    first, third = left * low, right * low
    top = jnp.concatenate([first, left - first, none, none], 0)
    bottom = jnp.concatenate([none, none, third, right - third], 0)
    return jnp.concatenate([top, bottom], 1)


def mul(a, b):
    return jnp.dot(a, b, preferred_element_type=F32)


WIDE = 2
LEAD = 236
GROUPS = 4


def gather_rows(q, lists_ref, cat_ref, rows_ref):
    for l in range(LANES):
        for r in range(2):
            rows_ref[q % (2 * WIDE), r, pl.ds(l, 1), :] = cat_ref[pl.ds(lists_ref[2 * q + r, l], 1), :]
        yield


def gram_pair(q, rows_ref, wgt_ref, first, work, consts):
    sq_ref, force_ref, scale_ref = work
    ident, lower, _, inflated = consts
    bounds = []
    rows = [rows_ref[q % (2 * WIDE), r] for r in range(2)]
    weighted = [(rows[r].T[:64] * wgt_ref[r, pl.ds(first + q, 1), :]).astype(BF16) for r in range(2)]
    yield
    grams = [mul(weighted[r], rows[r].astype(BF16)) for r in range(2)]
    yield
    for both in grams:
        total = jnp.sum(jnp.where(lower, jnp.abs(both), 0.0), axis=0, keepdims=True)
        bounds.append(inflated + jnp.max(total, axis=1, keepdims=True))
    turned = [pltpu.roll(x, 64, 1) for x in grams]
    inv = 1.0 / jnp.where(lower[:1], bounds[0], bounds[1])
    gram = jnp.where(lower, grams[0], turned[1])
    force = jnp.where(lower, turned[0], grams[1])
    sl = slice(q % 2 * 128, q % 2 * 128 + 128)
    sq_ref[q // 2, :, sl] = (gram + inflated * ident[:, :128]) * inv
    force_ref[q // 2, :, sl] = force.astype(BF16)
    scale_ref[q // 2, :, sl] = jnp.broadcast_to(inv, (8, 128))


def solve_stage(u, stage, held, work, consts, out_ref, first, members):
    state_ref, factor_ref = held
    sq_ref, force_ref, scale_ref = work
    ident, _, low, _ = consts
    last = 2 * NS_ITERS
    if stage == 0:
        h = (1.5 - SHIFT) * ident - 0.5 * sq_ref[u]
        product = mul(sq_ref[u].astype(BF16), block_diag(h.astype(BF16), low))
        yield
        state_ref[u, 64:] = SHIFT * ident + (1.5 - SHIFT) * ident - 0.5 * sq_ref[u]
        state_ref[u, :64] = SHIFT * sq_ref[u] + product
    elif stage < last - 1 and stage % 2 == 1:
        square = mul(state_ref[u, 64:].astype(BF16), block_diag(state_ref[u, :64].astype(BF16), low))
        yield
        factor_ref[u] = ((1.5 - SHIFT) * ident - 0.5 * square).astype(BF16)
    elif stage < last - 1:
        sl = slice(0 if stage < last - 2 else 64, 128)
        product = mul(state_ref[u, sl].astype(BF16), block_diag(factor_ref[u], low))
        yield
        state_ref[u, sl] = SHIFT * state_ref[u, sl] + product
    elif stage == last - 1:
        product = mul(state_ref[u, 64:].astype(BF16), block_diag(force_ref[u], low))
        yield
        factor_ref[u] = product.astype(BF16)
    else:
        shift = mul(state_ref[u, 64:].astype(BF16), block_diag(factor_ref[u], low))
        yield
        scale = scale_ref[u, :1]
        out_ref[first + u] = (math.sqrt(members - 1.0) * jnp.sqrt(scale)) * state_ref[u, 64:] + scale * shift


def run(steps, filler, share):
    for unit in steps:
        next(unit, None)
        for _ in range(share):
            next(filler, None)


def segment(stages, grams, filler):
    steps = grams + stages[0] + grams
    for i, (before, after) in enumerate(zip(stages[:-1], stages[1:])):
        for pair in zip(before, after):
            steps += pair
        if i == 0:
            steps += grams
    run(steps, filler, LEAD // len(steps))
    run(stages[-1], filler, (WIDE * LANES - LEAD) // len(stages[-1]) + 1)
    for _ in filler:
        pass


def transform_kernel(slot_ref, ens_ref, obs_ref, wgt_ref, lists_ref, out_ref, cat_ref, rows_ref, *scratch):
    work, (lists_a, lists_b, sems), held = (scratch[:3], scratch[3:6]), scratch[6:9], scratch[9:]
    smem = (lists_a, lists_b)
    groups = slot_ref.shape[0]
    _, windows, blocks, per, _ = ens_ref.shape
    members = groups * per
    count = lists_ref.shape[0]
    inflated = (members - 1) / INFL

    def fetch(b, half):
        return pltpu.make_async_copy(lists_ref.at[b], smem[half], sems.at[half])

    for half in range(2):
        fetch(half, half).start()

    def catalog(i, carry):
        w, b = i // blocks, i % blocks
        ens = jnp.concatenate([ens_ref[slot_ref[j], w, b].astype(F32) for j in range(groups)], 0)
        mean = jnp.sum(ens, axis=0, keepdims=True) * (1.0 / members)
        value = obs_ref[w, 0, pl.ds(b, 1), :]
        root = jnp.sqrt(obs_ref[w, 1, pl.ds(b, 1), :])
        anomaly = (ens - mean) * root
        innovation = jnp.broadcast_to((value - mean) * root, ens.shape)
        cat_ref[pl.ds(pl.multiple_of(i * LANES, LANES), LANES), :] = jnp.concatenate([anomaly, innovation], 0).T
        return carry

    lax.fori_loop(0, windows * blocks, catalog, 0, unroll=4)

    lower = lax.broadcasted_iota(jnp.int32, (64, 128), 1) < 64
    consts = (eye4(), lower, jnp.where(lower, 1.0, 0.0).astype(BF16), inflated)
    pairs = 2 * GROUPS
    last = 2 * NS_ITERS
    share = (last + 1) * WIDE // pairs

    def solve(stage, block, half):
        at = jnp.maximum(block, 0) * GROUPS
        return [solve_stage(u, stage, held, work[half], consts, out_ref, at, members) for u in range(GROUPS)]

    def gram(q, block, half):
        return gram_pair(q, rows_ref, wgt_ref, jnp.maximum(block, 0) * pairs, work[half], consts)

    def step(i, carry):
        for half in range(2):
            b = 2 * i + half
            for part in range(pairs // WIDE):

                @pl.when(slot_ref[0] >= 0)
                def _():
                    if part == 0:
                        fetch(b, half).wait()
                        stages = [solve(stage, b - 2, half) for stage in range(pairs // WIDE * share - share, last + 1)]
                        grams = [gram(q, b - 1, 1 - half) for q in range(pairs - WIDE, pairs)]
                    else:
                        stages = [solve(stage, b - 1, 1 - half) for stage in range(part * share - share, part * share)]
                        grams = [gram(q, b, half) for q in range((part - 1) * WIDE, part * WIDE)]
                    rows = [gather_rows(q, smem[half], cat_ref, rows_ref) for q in range(part * WIDE, (part + 1) * WIDE)]
                    segment(stages, grams, itertools.chain(*rows))

            @pl.when(b + 2 < count)
            def _():
                fetch(b + 2, half).start()

        return carry

    lax.fori_loop(0, count // 2, step, 0)

    def finish(units):
        for _ in range(3):
            run(units, iter(()), 0)

    for stage in range(pairs // WIDE * share - share, last + 1):
        finish(solve(stage, count - 2, 0))
    finish([gram(q, count - 1, 1) for q in range(pairs - WIDE, pairs)])
    for stage in range(last + 1):
        finish(solve(stage, count - 1, 1))


def transforms(slots, lists, ens, obs, wgt):
    columns = lists.shape[1]
    pairs = columns // 2
    _, windows, blocks, _, _ = ens.shape
    lists = lists.reshape(2, pairs // GROUPS, 2 * GROUPS, LANES).transpose(1, 2, 0, 3).reshape(-1, 4 * GROUPS, LANES)
    work = [
        pltpu.VMEM((GROUPS, 64, 256), F32),
        pltpu.VMEM((GROUPS, 64, 256), BF16),
        pltpu.VMEM((GROUPS, 8, 256), F32),
    ]
    return pl.pallas_call(
        transform_kernel,
        out_shape=jax.ShapeDtypeStruct((pairs, 64, 256), F32),
        in_specs=[SMEM] + [VMEM] * 4,
        out_specs=VMEM,
        scratch_shapes=[
            pltpu.VMEM((windows * blocks * LANES, LANES), F32),
            pltpu.VMEM((2 * WIDE, 2, LANES, LANES), F32),
            *work,
            *work,
            pltpu.SMEM((4 * GROUPS, LANES), jnp.int32),
            pltpu.SMEM((4 * GROUPS, LANES), jnp.int32),
            pltpu.SemaphoreType.DMA((2,)),
            pltpu.VMEM((GROUPS, 128, 256), F32),
            pltpu.VMEM((GROUPS, 64, 256), BF16),
        ],
        compiler_params=params(24),
        name="transforms",
    )(slots, ens, obs, wgt, lists)


def update_kernel(state_ref, transform_ref, out_ref, cells_ref, moved_ref, center_ref):
    groups, levels, _, tiles, per, _ = state_ref.shape
    width = tiles * LANES
    members = groups * per
    pairs = transform_ref.shape[0]

    def enter(z, carry):
        parts = []
        for r in range(2):
            blocks = [[state_ref[j, z, r, t].astype(F32) for j in range(groups)] for t in range(tiles)]
            state = jnp.concatenate([jnp.concatenate(b, 0) for b in blocks], 1)
            center = jnp.sum(state, axis=0, keepdims=True) * (1.0 / members)
            center_ref[z, pl.ds(r, 1), :] = center
            parts.append(state - center)
        cells_ref[pl.ds(pl.multiple_of(z * width, width), width), :] = jnp.concatenate(parts, 0).T
        return carry

    lax.fori_loop(0, levels, enter, 0, unroll=4)

    ident = eye4()
    lane = lax.broadcasted_iota(jnp.int32, (64, 128), 1)
    low = jnp.where(lane < 64, 1.0, 0.0).astype(BF16)

    def apply(g, carry):
        halves = []
        for half in range(2):
            q = g * 2 + half
            halves.append(jnp.concatenate([cells_ref[pl.ds(2 * q + c, levels, stride=width), :] for c in range(2)], 0))
        x = jnp.concatenate(halves, 1)
        t = transform_ref[g]
        on = t * ident
        diag = jnp.sum(on, axis=0, keepdims=True)
        y = x * diag + mul(x.astype(BF16), block_diag((t - on).astype(BF16), low))
        for half in range(2):
            q = g * 2 + half
            for c in range(2):
                moved_ref[pl.ds(2 * q + c, levels, stride=width), :] = y[c * levels : (c + 1) * levels, half * 128 : half * 128 + 128]
        return carry

    lax.fori_loop(0, pairs, apply, 0, unroll=4)

    def leave(z, carry):
        back = moved_ref[pl.ds(pl.multiple_of(z * width, width), width), :].T
        for r in range(2):
            out_ref[z, r] = (back[r * members : (r + 1) * members] + center_ref[z, pl.ds(r, 1), :]).astype(BF16)
        return carry

    lax.fori_loop(0, levels, leave, 0, unroll=4)


def update(state, transform):
    groups, levels, rows, tiles, per, _ = state.shape
    width = tiles * LANES
    return pl.pallas_call(
        update_kernel,
        out_shape=jax.ShapeDtypeStruct((levels, rows, groups * per, width), BF16),
        in_specs=[VMEM, VMEM],
        out_specs=VMEM,
        scratch_shapes=[
            pltpu.VMEM((levels * width, LANES), F32),
            pltpu.VMEM((levels * width, LANES), F32),
            pltpu.VMEM((levels, 8, width), F32),
        ],
        compiler_params=params(24),
        name="update",
    )(state, transform)


def cuts(levels):
    eighth = levels // 8
    ends = [0, eighth, 3 * eighth, 5 * eighth, 7 * eighth, levels]
    return list(zip(ends[:-1], ends[1:]))


def bit_reversed(value, bits):
    return sum(((value >> b) & 1) << (bits - 1 - b) for b in range(bits))


def on_device(prior, coefficients, measured, precision, location, lists, counts, loc_weight):
    slabs = lax.axis_size("slab")
    groups = lax.axis_size("mem")
    bits = groups.bit_length() - 1
    me = lax.axis_index("mem")
    up = [(i, i + 1) for i in range(slabs - 1)]
    down = [(i + 1, i) for i in range(slabs - 1)]
    swap = [(i, i ^ 1) for i in range(slabs)]
    skip = [(i, i + 2) for i in range(0, slabs - 2, 2)] + [(i, i - 2) for i in range(3, slabs, 2)]
    odd = lax.axis_index("slab") % 2 == 1
    columns = prior.shape[3]
    nobs = measured.shape[0]

    levels, members = prior.shape[1], prior.shape[0]
    own = jnp.transpose(prior, (1, 2, 0, 3))
    coef = jnp.transpose(coefficients, (0, 2, 1, 3))
    spans = cuts(levels)
    pieces = [own[first:last].reshape(-1, members, columns) for first, last in spans]
    flag = odd.astype(jnp.int32).reshape(1)
    share = levels // groups
    mine = lax.dynamic_slice_in_dim(coef, me * share, share, axis=2).astype(BF16)
    near = lax.ppermute(mine, "slab", swap)
    far = lax.ppermute(near, "slab", skip)
    sides = lax.all_gather(jnp.stack([near, far]), "mem", axis=0, tiled=False)
    cprev = jnp.where(odd, sides[:, 0, :, 1], sides[:, 1, :, 1]).astype(F32)
    cnext = jnp.where(odd, sides[:, 1, :, 0], sides[:, 0, :, 0]).astype(F32)

    besides, beyonds, fields = [], [], []

    def advance_piece(i):
        fields.append(forecast(spans[i], flag, pieces[i], besides[i], beyonds[i], coef, cprev, cnext))

    for i, piece in enumerate(pieces):
        if i == 2:
            far, piece = lax.optimization_barrier((far, piece))
        if i == 3:
            beyonds[0], piece = lax.optimization_barrier((beyonds[0], piece))
        if i >= 4:
            advance_piece(i - 4)
            fields[i - 4], beyonds[i - 3], piece = lax.optimization_barrier((fields[i - 4], beyonds[i - 3], piece))
        besides.append(lax.ppermute(piece, "slab", swap))
        if i >= 2:
            beyonds.append(lax.ppermute(besides[i - 2], "slab", skip))
    beyonds += [lax.ppermute(beside, "slab", skip) for beside in besides[-2:]]
    for i in range(len(fields), len(pieces)):
        advance_piece(i)

    zr, col = location // columns, location % columns
    block = zr * (columns // LANES) + col // LANES
    shift = (jnp.arange(nobs, dtype=jnp.int32) - col) % LANES
    seen = observe(block, shift, fields)
    extras = jnp.stack([measured, precision], 0)
    high = extras.astype(BF16)
    extras = jnp.concatenate([high, (extras - high.astype(F32)).astype(BF16)], 0)
    sent = jnp.concatenate([seen, extras.reshape((-1,) + seen.shape[1:])], 0)
    window = jnp.stack([lax.ppermute(sent, "slab", up), sent, lax.ppermute(sent, "slab", down)], 0)
    obs = window[:, seen.shape[0] :].reshape(3, 2, 2, nobs // LANES, LANES).astype(F32)
    obs = obs[:, 0] + obs[:, 1]
    window = window[:, : seen.shape[0]]
    tiles = columns // groups // LANES
    ship = jnp.concatenate(fields, 0)
    ship = jnp.transpose(ship.reshape(ship.shape[:2] + (groups, tiles) + ship.shape[3:]), (2, 0, 1, 3, 4, 5))
    ens = window[None]
    distance = groups // 2
    while distance:
        ens = jnp.concatenate([ens, lax.ppermute(ens, "mem", [(i, i ^ distance) for i in range(groups)])], 0)
        if distance == groups // 2:
            ens, ship = lax.optimization_barrier((ens, ship))
        distance //= 2
    slots = bit_reversed(jnp.arange(groups, dtype=jnp.int32) ^ me, bits)

    position = lax.broadcasted_iota(jnp.int32, loc_weight.shape, 2)
    wgt = jnp.where(position < counts[..., None], loc_weight, 0.0)
    transform = transforms(slots, lists, ens, obs, wgt)

    ship, _ = lax.optimization_barrier((ship, ens))
    state = lax.all_to_all(ship, "mem", 0, 0, tiled=False)
    result = update(state, transform)
    return jnp.transpose(result, (2, 0, 1, 3))


def solution(mesh):
    return jax.shard_map(
        on_device,
        mesh=mesh,
        in_specs=(
            P("mem", None, "slab", None),
            P(None, None, "slab", None),
            P("slab"),
            P("slab"),
            P("slab"),
            P("slab", "mem", None),
            P("slab", "mem"),
            P("slab", "mem", None),
        ),
        out_specs=P(None, None, "slab", "mem"),
        check_vma=False,
    )
```

```python
import functools
import itertools
import math

import jax
import jax.numpy as jnp
from jax import lax
from jax.experimental import pallas as pl
from jax.experimental.pallas import tpu as pltpu
from jax.sharding import PartitionSpec as P

NS_ITERS = 4
INFL = 1.1
SHIFT = 1.25
LANES = 128
F32 = jnp.float32
BF16 = jnp.bfloat16
VMEM = pl.BlockSpec(memory_space=pltpu.VMEM)
SMEM = pl.BlockSpec(memory_space=pltpu.SMEM)


def params(mib):
    return pltpu.CompilerParams(vmem_limit_bytes=mib * 1024 * 1024)


def advance(upper, lower, center, w):
    width = center.shape[1]
    east = pltpu.roll(center, width - 1, 1)
    west = pltpu.roll(center, 1, 1)
    return w[0] * center + w[1] * upper + w[2] * lower + w[3] * east + w[4] * west


def weights(c):
    across, along = 0.5 * c[0], 0.5 * c[1]
    return [1.0 - 4.0 * c[2], c[2] - across, c[2] + across, c[2] - along, c[2] + along]


def forecast_kernel(first, odd_ref, own_ref, beside_ref, beyond_ref, coef_ref, cprev_ref, cnext_ref, field_ref, weight_ref):
    levels, width = field_ref.shape[0], own_ref.shape[2]
    odd = odd_ref[0] == 1
    share = cprev_ref.shape[2]
    for block in range(first // share, (first + levels - 1) // share + 1):
        low, high = max(block * share, first), min(block * share + share, first + levels)
        inner = slice(low - block * share, high - block * share)
        for row in range(4):
            if row in (1, 2):
                c = [coef_ref[k, row - 1, low:high, :] for k in range(3)]
            else:
                side_ref = cprev_ref if row == 0 else cnext_ref
                c = [side_ref[block, k, inner, :] for k in range(3)]
            for i, w in enumerate(weights(c)):
                weight_ref[row * 5 + i, low - first : high - first, :] = w

    def level(z, carry):
        beside = [beside_ref[2 * z + r].astype(F32) for r in range(2)]
        beyond = [beyond_ref[2 * z + r].astype(F32) for r in range(2)]
        rows = [jnp.where(odd, beside[r], beyond[r]) for r in range(2)]
        rows += [own_ref[2 * z + r].astype(F32) for r in range(2)]
        rows += [jnp.where(odd, beyond[r], beside[r]) for r in range(2)]
        at = pl.ds(z, 1)
        w = [[weight_ref[row * 5 + i, at, :] for i in range(5)] for row in range(4)]
        once = [advance(rows[i + 2], rows[i], rows[i + 1], w[i]) for i in range(4)]
        for r in range(2):
            twice = advance(once[r + 2], once[r], once[r + 1], w[r + 1]).astype(BF16)
            for t in range(width // LANES):
                field_ref[z, r, t] = twice[:, t * LANES : (t + 1) * LANES]
        return carry

    lax.fori_loop(0, levels, level, 0)


def forecast(span, odd, own, beside, beyond, coef, cprev, cnext):
    first, levels, rows = span[0], span[1] - span[0], coef.shape[1]
    _, members, width = own.shape
    return pl.pallas_call(
        functools.partial(forecast_kernel, first),
        out_shape=jax.ShapeDtypeStruct((levels, rows, width // LANES, members, LANES), BF16),
        in_specs=[SMEM] + [VMEM] * 6,
        out_specs=VMEM,
        scratch_shapes=[pltpu.VMEM((20, levels, width), F32)],
        compiler_params=params(32),
        name="forecast",
    )(odd, own, beside, beyond, coef, cprev, cnext)


BATCH = 4


def observe_kernel(index_ref, *refs):
    *part_refs, out_ref, field_ref, smem_a, smem_b, sems = refs
    smem = (smem_a, smem_b)
    count = index_ref.shape[0]
    members = out_ref.shape[1]
    lane = lax.broadcasted_iota(jnp.int32, (members, LANES), 1)

    def fetch(b, half):
        return pltpu.make_async_copy(index_ref.at[b], smem[half], sems.at[half])

    for half in range(2):
        fetch(half, half).start()
    first = 0
    for part in part_refs:
        field_ref[first : first + part.shape[0]] = part[...]
        first += part.shape[0]

    def pair(i, carry):
        for half in range(2):
            b = 2 * i + half
            fetch(b, half).wait()
            for j in range(BATCH):
                acc = jnp.zeros((members, LANES), F32)
                for o in range(LANES):
                    tile = field_ref[smem[half][2 * j, o]].astype(F32)
                    acc = jnp.where(lane == o, pltpu.roll(tile, smem[half][2 * j + 1, o], 1), acc)
                out_ref[b * BATCH + j] = acc.astype(BF16)

            @pl.when(b + 2 < count)
            def _():
                fetch(b + 2, half).start()

        return carry

    lax.fori_loop(0, count // 2, pair, 0)


def observe(block, shift, fields):
    parts = [f.reshape((-1,) + f.shape[3:]) for f in fields]
    members = parts[0].shape[1]
    index = jnp.stack([block.reshape(-1, LANES), shift.reshape(-1, LANES)], 1).reshape(-1, 2 * BATCH, LANES)
    return pl.pallas_call(
        observe_kernel,
        out_shape=jax.ShapeDtypeStruct((block.shape[0] // LANES, members, LANES), BF16),
        in_specs=[VMEM] + [VMEM] * len(parts),
        out_specs=VMEM,
        scratch_shapes=[
            pltpu.VMEM((sum(p.shape[0] for p in parts), members, LANES), BF16),
            pltpu.SMEM((2 * BATCH, LANES), jnp.int32),
            pltpu.SMEM((2 * BATCH, LANES), jnp.int32),
            pltpu.SemaphoreType.DMA((2,)),
        ],
        compiler_params=params(32),
        name="observe",
    )(index, *parts)


def eye4():
    row = lax.broadcasted_iota(jnp.int32, (64, 256), 0)
    lane = lax.broadcasted_iota(jnp.int32, (64, 256), 1)
    return jnp.where(row == lane % 64, 1.0, 0.0).astype(F32)


def block_diag(x, low):
    left, right = x[:, :128], x[:, 128:]
    none = jnp.zeros_like(left)
    first, third = left * low, right * low
    top = jnp.concatenate([first, left - first, none, none], 0)
    bottom = jnp.concatenate([none, none, third, right - third], 0)
    return jnp.concatenate([top, bottom], 1)


def mul(a, b):
    return jnp.dot(a, b, preferred_element_type=F32)


WIDE = 2
LEAD = 236
GROUPS = 4


def gather_rows(q, lists_ref, cat_ref, rows_ref):
    for l in range(LANES):
        for r in range(2):
            rows_ref[q % (2 * WIDE), r, pl.ds(l, 1), :] = cat_ref[pl.ds(lists_ref[2 * q + r, l], 1), :]
        yield


def gram_pair(q, rows_ref, wgt_ref, first, work, consts):
    sq_ref, force_ref, scale_ref = work
    ident, lower, _, inflated = consts
    bounds = []
    rows = [rows_ref[q % (2 * WIDE), r] for r in range(2)]
    weighted = [(rows[r].T[:64] * wgt_ref[r, pl.ds(first + q, 1), :]).astype(BF16) for r in range(2)]
    yield
    grams = [mul(weighted[r], rows[r].astype(BF16)) for r in range(2)]
    yield
    for both in grams:
        total = jnp.sum(jnp.where(lower, jnp.abs(both), 0.0), axis=0, keepdims=True)
        bounds.append(inflated + jnp.max(total, axis=1, keepdims=True))
    turned = [pltpu.roll(x, 64, 1) for x in grams]
    inv = 1.0 / jnp.where(lower[:1], bounds[0], bounds[1])
    gram = jnp.where(lower, grams[0], turned[1])
    force = jnp.where(lower, turned[0], grams[1])
    sl = slice(q % 2 * 128, q % 2 * 128 + 128)
    sq_ref[q // 2, :, sl] = (gram + inflated * ident[:, :128]) * inv
    force_ref[q // 2, :, sl] = force.astype(BF16)
    scale_ref[q // 2, :, sl] = jnp.broadcast_to(inv, (8, 128))


def solve_stage(u, stage, held, work, consts, out_ref, diag_ref, first, members):
    state_ref, factor_ref = held
    sq_ref, force_ref, scale_ref = work
    ident, _, low, _ = consts
    last = 2 * NS_ITERS
    if stage == 0:
        h = (1.5 - SHIFT) * ident - 0.5 * sq_ref[u]
        product = mul(sq_ref[u].astype(BF16), block_diag(h.astype(BF16), low))
        yield
        state_ref[u, 64:] = SHIFT * ident + (1.5 - SHIFT) * ident - 0.5 * sq_ref[u]
        state_ref[u, :64] = SHIFT * sq_ref[u] + product
    elif stage < last - 1 and stage % 2 == 1:
        square = mul(state_ref[u, 64:].astype(BF16), block_diag(state_ref[u, :64].astype(BF16), low))
        yield
        factor_ref[u] = ((1.5 - SHIFT) * ident - 0.5 * square).astype(BF16)
    elif stage < last - 1:
        sl = slice(0 if stage < last - 2 else 64, 128)
        product = mul(state_ref[u, sl].astype(BF16), block_diag(factor_ref[u], low))
        yield
        state_ref[u, sl] = SHIFT * state_ref[u, sl] + product
    elif stage == last - 1:
        product = mul(state_ref[u, 64:].astype(BF16), block_diag(force_ref[u], low))
        yield
        factor_ref[u] = product.astype(BF16)
    else:
        shift = mul(state_ref[u, 64:].astype(BF16), block_diag(factor_ref[u], low))
        yield
        scale = scale_ref[u, :1]
        transform = (math.sqrt(members - 1.0) * jnp.sqrt(scale)) * state_ref[u, 64:] + scale * shift
        on = transform * ident
        out_ref[first + u] = (transform - on).astype(BF16)
        diag_ref[first + u] = jnp.broadcast_to(jnp.sum(on, axis=0, keepdims=True), (8, 256))


def run(steps, filler, share):
    for unit in steps:
        next(unit, None)
        for _ in range(share):
            next(filler, None)


def segment(stages, grams, filler):
    steps = grams + stages[0] + grams
    for i, (before, after) in enumerate(zip(stages[:-1], stages[1:])):
        for pair in zip(before, after):
            steps += pair
        if i == 0:
            steps += grams
    run(steps, filler, LEAD // len(steps))
    run(stages[-1], filler, (WIDE * LANES - LEAD) // len(stages[-1]) + 1)
    for _ in filler:
        pass


def transform_kernel(slot_ref, ens_ref, obs_ref, wgt_ref, lists_ref, out_ref, diag_ref, cat_ref, rows_ref, *scratch):
    work, (lists_a, lists_b, sems), held = (scratch[:3], scratch[3:6]), scratch[6:9], scratch[9:]
    smem = (lists_a, lists_b)
    groups = slot_ref.shape[0]
    _, windows, blocks, per, _ = ens_ref.shape
    members = groups * per
    count = lists_ref.shape[0]
    inflated = (members - 1) / INFL

    def fetch(b, half):
        return pltpu.make_async_copy(lists_ref.at[b], smem[half], sems.at[half])

    for half in range(2):
        fetch(half, half).start()

    def catalog(i, carry):
        w, b = i // blocks, i % blocks
        ens = jnp.concatenate([ens_ref[slot_ref[j], w, b].astype(F32) for j in range(groups)], 0)
        mean = jnp.sum(ens, axis=0, keepdims=True) * (1.0 / members)
        value = obs_ref[w, 0, pl.ds(b, 1), :]
        root = jnp.sqrt(obs_ref[w, 1, pl.ds(b, 1), :])
        anomaly = (ens - mean) * root
        innovation = jnp.broadcast_to((value - mean) * root, ens.shape)
        cat_ref[pl.ds(pl.multiple_of(i * LANES, LANES), LANES), :] = jnp.concatenate([anomaly, innovation], 0).T
        return carry

    lax.fori_loop(0, windows * blocks, catalog, 0, unroll=4)

    lower = lax.broadcasted_iota(jnp.int32, (64, 128), 1) < 64
    consts = (eye4(), lower, jnp.where(lower, 1.0, 0.0).astype(BF16), inflated)
    pairs = 2 * GROUPS
    last = 2 * NS_ITERS
    share = (last + 1) * WIDE // pairs

    def solve(stage, block, half):
        at = jnp.maximum(block, 0) * GROUPS
        return [solve_stage(u, stage, held, work[half], consts, out_ref, diag_ref, at, members) for u in range(GROUPS)]

    def gram(q, block, half):
        return gram_pair(q, rows_ref, wgt_ref, jnp.maximum(block, 0) * pairs, work[half], consts)

    def step(i, carry):
        for half in range(2):
            b = 2 * i + half
            for part in range(pairs // WIDE):

                @pl.when(slot_ref[0] >= 0)
                def _():
                    if part == 0:
                        fetch(b, half).wait()
                        stages = [solve(stage, b - 2, half) for stage in range(pairs // WIDE * share - share, last + 1)]
                        grams = [gram(q, b - 1, 1 - half) for q in range(pairs - WIDE, pairs)]
                    else:
                        stages = [solve(stage, b - 1, 1 - half) for stage in range(part * share - share, part * share)]
                        grams = [gram(q, b, half) for q in range((part - 1) * WIDE, part * WIDE)]
                    rows = [gather_rows(q, smem[half], cat_ref, rows_ref) for q in range(part * WIDE, (part + 1) * WIDE)]
                    segment(stages, grams, itertools.chain(*rows))

            @pl.when(b + 2 < count)
            def _():
                fetch(b + 2, half).start()

        return carry

    lax.fori_loop(0, count // 2, step, 0)

    def finish(units):
        for _ in range(3):
            run(units, iter(()), 0)

    for stage in range(pairs // WIDE * share - share, last + 1):
        finish(solve(stage, count - 2, 0))
    finish([gram(q, count - 1, 1) for q in range(pairs - WIDE, pairs)])
    for stage in range(last + 1):
        finish(solve(stage, count - 1, 1))


def transforms(slots, lists, ens, obs, wgt):
    columns = lists.shape[1]
    pairs = columns // 2
    _, windows, blocks, _, _ = ens.shape
    lists = lists.reshape(2, pairs // GROUPS, 2 * GROUPS, LANES).transpose(1, 2, 0, 3).reshape(-1, 4 * GROUPS, LANES)
    work = [
        pltpu.VMEM((GROUPS, 64, 256), F32),
        pltpu.VMEM((GROUPS, 64, 256), BF16),
        pltpu.VMEM((GROUPS, 8, 256), F32),
    ]
    return pl.pallas_call(
        transform_kernel,
        out_shape=[
            jax.ShapeDtypeStruct((pairs, 64, 256), BF16),
            jax.ShapeDtypeStruct((pairs, 8, 256), F32),
        ],
        in_specs=[SMEM] + [VMEM] * 4,
        out_specs=[VMEM] * 2,
        scratch_shapes=[
            pltpu.VMEM((windows * blocks * LANES, LANES), F32),
            pltpu.VMEM((2 * WIDE, 2, LANES, LANES), F32),
            *work,
            *work,
            pltpu.SMEM((4 * GROUPS, LANES), jnp.int32),
            pltpu.SMEM((4 * GROUPS, LANES), jnp.int32),
            pltpu.SemaphoreType.DMA((2,)),
            pltpu.VMEM((GROUPS, 128, 256), F32),
            pltpu.VMEM((GROUPS, 64, 256), BF16),
        ],
        compiler_params=params(24),
        name="transforms",
    )(slots, ens, obs, wgt, lists)


def update_kernel(state_ref, transform_ref, diag_ref, out_ref, cells_ref, moved_ref, center_ref):
    groups, levels, _, tiles, per, _ = state_ref.shape
    width = tiles * LANES
    members = groups * per
    pairs = transform_ref.shape[0]

    def enter(z, carry):
        parts = []
        for r in range(2):
            blocks = [[state_ref[j, z, r, t].astype(F32) for j in range(groups)] for t in range(tiles)]
            state = jnp.concatenate([jnp.concatenate(b, 0) for b in blocks], 1)
            center = jnp.sum(state, axis=0, keepdims=True) * (1.0 / members)
            center_ref[z, pl.ds(r, 1), :] = center
            parts.append(state - center)
        cells_ref[pl.ds(pl.multiple_of(z * width, width), width), :] = jnp.concatenate(parts, 0).T
        return carry

    lax.fori_loop(0, levels, enter, 0, unroll=4)

    lane = lax.broadcasted_iota(jnp.int32, (64, 128), 1)
    low = jnp.where(lane < 64, 1.0, 0.0).astype(BF16)

    def apply(g, carry):
        halves = []
        for half in range(2):
            q = g * 2 + half
            halves.append(jnp.concatenate([cells_ref[pl.ds(2 * q + c, levels, stride=width), :] for c in range(2)], 0))
        x = jnp.concatenate(halves, 1)
        y = x * diag_ref[g, :1] + mul(x.astype(BF16), block_diag(transform_ref[g], low))
        for half in range(2):
            q = g * 2 + half
            for c in range(2):
                moved_ref[pl.ds(2 * q + c, levels, stride=width), :] = y[c * levels : (c + 1) * levels, half * 128 : half * 128 + 128]
        return carry

    lax.fori_loop(0, pairs, apply, 0, unroll=4)

    def leave(z, carry):
        back = moved_ref[pl.ds(pl.multiple_of(z * width, width), width), :].T
        for r in range(2):
            out_ref[z, r] = (back[r * members : (r + 1) * members] + center_ref[z, pl.ds(r, 1), :]).astype(BF16)
        return carry

    lax.fori_loop(0, levels, leave, 0, unroll=4)


def update(state, transform, diag):
    groups, levels, rows, tiles, per, _ = state.shape
    width = tiles * LANES
    return pl.pallas_call(
        update_kernel,
        out_shape=jax.ShapeDtypeStruct((levels, rows, groups * per, width), BF16),
        in_specs=[VMEM] * 3,
        out_specs=VMEM,
        scratch_shapes=[
            pltpu.VMEM((levels * width, LANES), F32),
            pltpu.VMEM((levels * width, LANES), F32),
            pltpu.VMEM((levels, 8, width), F32),
        ],
        compiler_params=params(24),
        name="update",
    )(state, transform, diag)


def cuts(levels):
    eighth = levels // 8
    ends = [0, eighth, 3 * eighth, 5 * eighth, 7 * eighth, levels]
    return list(zip(ends[:-1], ends[1:]))


def bit_reversed(value, bits):
    return sum(((value >> b) & 1) << (bits - 1 - b) for b in range(bits))


def on_device(prior, coefficients, measured, precision, location, lists, counts, loc_weight):
    slabs = lax.axis_size("slab")
    groups = lax.axis_size("mem")
    bits = groups.bit_length() - 1
    me = lax.axis_index("mem")
    up = [(i, i + 1) for i in range(slabs - 1)]
    down = [(i + 1, i) for i in range(slabs - 1)]
    swap = [(i, i ^ 1) for i in range(slabs)]
    skip = [(i, i + 2) for i in range(0, slabs - 2, 2)] + [(i, i - 2) for i in range(3, slabs, 2)]
    odd = lax.axis_index("slab") % 2 == 1
    columns = prior.shape[3]
    nobs = measured.shape[0]

    levels, members = prior.shape[1], prior.shape[0]
    own = jnp.transpose(prior, (1, 2, 0, 3))
    coef = jnp.transpose(coefficients, (0, 2, 1, 3))
    spans = cuts(levels)
    pieces = [own[first:last].reshape(-1, members, columns) for first, last in spans]
    flag = odd.astype(jnp.int32).reshape(1)
    share = levels // groups
    mine = lax.dynamic_slice_in_dim(coef, me * share, share, axis=2).astype(BF16)
    near = lax.ppermute(mine, "slab", swap)
    far = lax.ppermute(near, "slab", skip)
    sides = lax.all_gather(jnp.stack([near, far]), "mem", axis=0, tiled=False)
    cprev = jnp.where(odd, sides[:, 0, :, 1], sides[:, 1, :, 1]).astype(F32)
    cnext = jnp.where(odd, sides[:, 1, :, 0], sides[:, 0, :, 0]).astype(F32)

    besides, beyonds, fields = [], [], []

    def advance_piece(i):
        fields.append(forecast(spans[i], flag, pieces[i], besides[i], beyonds[i], coef, cprev, cnext))

    for i, piece in enumerate(pieces):
        if i == 2:
            far, piece = lax.optimization_barrier((far, piece))
        if i == 3:
            beyonds[0], piece = lax.optimization_barrier((beyonds[0], piece))
        if i >= 4:
            advance_piece(i - 4)
            fields[i - 4], beyonds[i - 3], piece = lax.optimization_barrier((fields[i - 4], beyonds[i - 3], piece))
        besides.append(lax.ppermute(piece, "slab", swap))
        if i >= 2:
            beyonds.append(lax.ppermute(besides[i - 2], "slab", skip))
    beyonds += [lax.ppermute(beside, "slab", skip) for beside in besides[-2:]]
    for i in range(len(fields), len(pieces)):
        advance_piece(i)

    zr, col = location // columns, location % columns
    block = zr * (columns // LANES) + col // LANES
    shift = (jnp.arange(nobs, dtype=jnp.int32) - col) % LANES
    seen = observe(block, shift, fields)
    extras = jnp.stack([measured, precision], 0)
    high = extras.astype(BF16)
    extras = jnp.concatenate([high, (extras - high.astype(F32)).astype(BF16)], 0)
    sent = jnp.concatenate([seen, extras.reshape((-1,) + seen.shape[1:])], 0)
    window = jnp.stack([lax.ppermute(sent, "slab", up), sent, lax.ppermute(sent, "slab", down)], 0)
    obs = window[:, seen.shape[0] :].reshape(3, 2, 2, nobs // LANES, LANES).astype(F32)
    obs = obs[:, 0] + obs[:, 1]
    window = window[:, : seen.shape[0]]
    tiles = columns // groups // LANES
    ship = jnp.concatenate(fields, 0)
    ship = jnp.transpose(ship.reshape(ship.shape[:2] + (groups, tiles) + ship.shape[3:]), (2, 0, 1, 3, 4, 5))
    ens = window[None]
    distance = groups // 2
    while distance:
        arrived = lax.ppermute(ens, "mem", [(i, i ^ distance) for i in range(groups)])
        arrived, ship = lax.optimization_barrier((arrived, ship))
        ens = jnp.concatenate([ens, arrived], 0)
        distance //= 2
    slots = bit_reversed(jnp.arange(groups, dtype=jnp.int32) ^ me, bits)

    position = lax.broadcasted_iota(jnp.int32, loc_weight.shape, 2)
    wgt = jnp.where(position < counts[..., None], loc_weight, 0.0)
    transform, diag = transforms(slots, lists, ens, obs, wgt)

    state = lax.all_to_all(ship, "mem", 0, 0, tiled=False)
    result = update(state, transform, diag)
    return jnp.transpose(result, (2, 0, 1, 3))


def solution(mesh):
    return jax.shard_map(
        on_device,
        mesh=mesh,
        in_specs=(
            P("mem", None, "slab", None),
            P(None, None, "slab", None),
            P("slab"),
            P("slab"),
            P("slab"),
            P("slab", "mem", None),
            P("slab", "mem"),
            P("slab", "mem", None),
        ),
        out_specs=P(None, None, "slab", "mem"),
        check_vma=False,
    )
```
